256 devices in a mesh: dp: 32 (over y, x, core), tr: 2 (over z_lo), tc: 4 (over z_hi).
Axes of the slice: x: 4, y: 4, z: 8 (z_hi: 4, z_lo: 2; z = z_hi * 2 + z_lo), core: 2. Of those that a mesh axis runs over, the one named last changes fastest.
Arguments:
- activations: bfloat16 [32768, 3072], P(('dp', 'tc'), 'tr'), may hold values from -24 to 24
- cotangent: bfloat16 [32768, 8192], P(('dp', 'tr'), 'tc'), may hold values from -0.03125 to 0.03125
- master: float32 [2, 1536, 8192], P('tr', ('dp', 'tc')), may hold values from -3 to 3
- moment: float32 [2, 1536, 8192], P('tr', ('dp', 'tc')), may hold values from -2 to 2
- second: float32 [2, 1536, 8192], P('tr', ('dp', 'tc')), may hold values from 0.05 to 2
Outputs:
- new_master: float32 [2, 1536, 8192], P('tr', ('dp', 'tc'))
- new_moment: float32 [2, 1536, 8192], P('tr', ('dp', 'tc'))
- new_second: float32 [2, 1536, 8192], P('tr', ('dp', 'tc'))
The draws below stay inside these ranges and needn't reach their ends.
All inputs are finite; a program needn't handle non-finite values.
Results may differ from the reference program's by a relative error of at most 0.0003.
Values may be sent and summed in bfloat16 or wider, within the bound.
No kernel may reach another device: no remote copies, remote signals or barrier semaphores. Data moves between devices by JAX's collectives and lax.ppermute only.
A program may use at most 128 MiB of HBM per device.

```python
import math
import jax
import jax.numpy as jnp
from jax import lax

D = 3072
FFW = 8192
TOK_REP = 1024
TOKENS = 32768
N_DP = 32
N_TR = 2


def strengthened(array, stream_key, source, target, parts, factor):
    def block_of(position):
        return (jnp.arange(array.shape[position]) // (array.shape[position] // parts)).reshape((-1,) + (1,) * (array.ndim - 1 - position))

    one_side = jax.random.permutation(stream_key, parts)[block_of(target)]
    second = (block_of(target) + parts // 2) % parts
    return jnp.where((block_of(source) == one_side) | (block_of(source) == second), factor * array, array)


def level_of(key, dims, shards, least, largest):
    def one(position, blocks):
        heights = jax.random.uniform(jax.random.fold_in(jax.random.fold_in(key, 6), position), (blocks,), jnp.float32, least / len(shards), largest / len(shards))
        return jnp.repeat(jnp.exp(heights), dims[position] // blocks).reshape((-1,) + (1,) * (len(dims) - position - 1))

    level = one(*shards[0])
    for cut in shards[1:]:
        level = level * one(*cut)
    return level


def centred(rng, shape, width, reach, shards=(), dtype=jnp.bfloat16):
    array = width * jax.random.normal(rng, shape, jnp.float32)
    if shards:
        array = array * level_of(rng, shape, shards, -0.22, 0.18)
    return jnp.clip(array, -reach, reach).astype(dtype)


def heavy_noise(stream_key, shape, width, limit, cuts, heavy, held_as=jnp.bfloat16):
    drawn = width * jax.random.normal(stream_key, shape, jnp.float32)
    if cuts:
        drawn = drawn * level_of(stream_key, shape, cuts, -0.22, 0.18)
    return jnp.clip(strengthened(drawn, jax.random.fold_in(stream_key, 3), *heavy), -limit, limit).astype(held_as)


def setup_inputs(seed: int = 0) -> dict:
    key_of = jax.random.split(jax.random.key(seed), 6)
    return {
        "activations": heavy_noise(key_of[0], (TOKENS, D), 1.0, 24.0, ((0, 128), (1, 2)), (0, 1, 128, 5.5)),
        "cotangent": centred(key_of[1], (TOKENS, FFW), TOKENS ** -0.5, 0.03125, ((0, 64), (1, 4))),
        "master": centred(key_of[2], (N_TR, D // N_TR, FFW), 0.5, 3.0, ((0, 2), (1, 128)), jnp.float32),
        "moment": centred(key_of[3], (N_TR, D // N_TR, FFW), 0.3, 2.0, ((0, 2), (1, 128)), jnp.float32),
        "second": jnp.clip(jnp.exp(math.log(2.0) - 3.6888794 * jax.random.uniform(key_of[4], (N_TR, D // N_TR, FFW), jnp.float32) ** level_of(key_of[4], (N_TR, D // N_TR, FFW), ((0, 2), (1, 128)), -0.2, 0.2)), 0.05, 2.0),
    }


first_decay = 0.9
second_decay = 0.95
learn_rate = 0.0003
weight_decay = 0.1
epsilon = 1e-08
first_fix = 1.0 - 0.9 ** 10
second_fix = 1.0 - 0.95 ** 10

def reference(activations, cotangent, master, moment, second):
    blocks_x = activations.reshape(N_DP, TOK_REP, D)
    blocks_y = cotangent.reshape(N_DP, TOK_REP, FFW)

    def accumulate(total, pair):
        return (total + jnp.dot(pair[0].T, pair[1], preferred_element_type=jnp.float32), None)
    grad, unused = lax.scan(accumulate, jnp.zeros((D, FFW), jnp.float32), (blocks_x, blocks_y))
    grad = grad.reshape(N_TR, D // N_TR, FFW)
    new_moment = first_decay * moment + (1.0 - first_decay) * grad
    new_second = second_decay * second + (1.0 - second_decay) * grad * grad
    update = new_moment / first_fix / (jnp.sqrt(new_second / second_fix) + epsilon)
    new_master = master - learn_rate * (update + weight_decay * master)
    return (new_master, new_moment, new_second)
```

```python
import jax
import jax.numpy as jnp
from jax import lax
from jax.experimental import pallas as pl
from jax.experimental.pallas import tpu as pltpu
from jax.sharding import PartitionSpec as P

first_decay = 0.9
second_decay = 0.95
learn_rate = 0.0003
weight_decay = 0.1
epsilon = 1e-08
first_fix = 1.0 - 0.9**10
second_fix = 1.0 - 0.95**10

AXES = ("dp", "tr", "tc")
SIDE = 4
ROWS = 48
CHUNKS = (24, 24)


def moves(where):
    pairs = []
    for dp in range(32):
        for tr in range(2):
            for tc in range(4):
                y, x, core, z = where(dp // 8, dp // 2 % 4, dp % 2, 2 * tc + tr)
                to = (y % 4 * 8 + x % 4 * 2 + core % 2, z % 2, z % 8 // 2)
                pairs.append(((dp * 2 + tr) * 4 + tc, (to[0] * 2 + to[1]) * 4 + to[2]))
    return pairs


def step(first, sign):
    def where(y, x, core, z):
        if (core == 0) == first:
            return y, x + sign, core, z
        return y + sign, x, core, z

    return moves(where)


def send(array, pairs):
    return lax.ppermute(array, AXES, pairs)


OTHER_CORE = moves(lambda y, x, core, z: (y, x, 1 - core, z))
PAIR = moves(lambda y, x, core, z: (y, x, core, z ^ 1))


def feature_order(activations):
    dp = lax.axis_index("dp")
    my_y, my_x, core = dp // 8, dp // 2 % 4, dp % 2
    column = lax.broadcasted_iota(jnp.int32, (1, 2 * SIDE * SIDE * ROWS), 1)
    half, rest = column // (SIDE * SIDE * ROWS), column % (SIDE * SIDE * ROWS)
    target = jnp.where(half == 0, core, 1 - core)
    source = jnp.zeros_like(column)
    start = 0
    for rows in CHUNKS:
        size = SIDE * SIDE * rows
        inside = rest - start * SIDE * SIDE
        near, far, row = inside // (SIDE * rows), inside // rows % SIDE, inside % rows
        x = jnp.where(target == 0, my_x + near, my_x + far) % SIDE
        y = jnp.where(target == 0, my_y + far, my_y + near) % SIDE
        feature = (y * SIDE + x) * 2 * ROWS + target * ROWS + start + row
        source = jnp.where((inside >= 0) & (inside < size), feature, source)
        start += rows
    feature = lax.broadcasted_iota(jnp.int32, (activations.shape[1], column.shape[1]), 0)
    chosen = (feature == source).astype(activations.dtype)
    return jnp.dot(activations, chosen, preferred_element_type=jnp.float32).astype(activations.dtype)


def product_kernel(act, own_keep, own_came, far_keep, far_came, plus, minus, add_plus, add_minus, mine):
    tr = lax.axis_index("tr")
    features = act.shape[-1]

    def part(half, replica, cot):
        rows = act[pl.ds(2 * half, 2), 0, replica].reshape(cot.shape[0], features)
        return lax.dot_general(rows, cot[...], (((0,), (0,)), ((), ())), preferred_element_type=jnp.float32)

    total = part(tr, 0, own_keep) + part(1 - tr, 0, own_came)
    total = total + (part(tr, 1, far_keep) + part(1 - tr, 1, far_came))
    total = total.reshape(SIDE, SIDE, 1, features // SIDE**2, total.shape[-1])
    plus[0] = total[2, :2]
    plus[1] = total[1, 2:]
    minus[0] = total[2, 2:]
    minus[1] = total[3, :2]
    add_plus[...] = total[1, :2]
    add_minus[...] = total[3, 2:]
    mine[...] = total[0]


def product(act, cots):
    features, units = act.shape[-1], cots[0].shape[1]
    rows = features // SIDE**2
    whole = pl.BlockSpec(cots[0].shape, lambda i: (0, 0))
    lead = pl.BlockSpec((2, 2, 1, rows, units), lambda i: (0, 0, i, 0, 0))
    pack = pl.BlockSpec((2, 2, 1, rows, units), lambda i: (0, 0, i, 0, 0))
    part = pl.BlockSpec((2, 1, rows, units), lambda i: (0, i, 0, 0))
    full = pl.BlockSpec((SIDE, 1, rows, units), lambda i: (0, i, 0, 0))
    packed = jax.ShapeDtypeStruct((2, 2, 2, rows, units), jnp.float32)
    parted = jax.ShapeDtypeStruct((2, 2, rows, units), jnp.float32)
    return pl.pallas_call(
        product_kernel,
        grid=(2,),
        in_specs=[pl.BlockSpec((4, 1, 2, act.shape[3], features), lambda i: (0, i, 0, 0, 0))] + [whole] * 4,
        out_specs=[lead, pack, part, part, full],
        out_shape=[packed, packed, parted, parted, jax.ShapeDtypeStruct((SIDE, 2, rows, units), jnp.float32)],
        compiler_params=pltpu.CompilerParams(vmem_limit_bytes=40 * 2**20),
        cost_estimate=pl.CostEstimate(
            flops=2 * 2 * features * 4 * cots[0].shape[0] * units, bytes_accessed=12 * 2**20, transcendentals=0
        ),
    )(act, *cots)


def summed(parts):
    plus, minus, add_plus, add_minus, mine = parts
    left = send(plus, step(True, 1))
    right = send(minus, step(True, -1))
    near = send(add_plus + left[0], step(True, 1))
    far = send(add_minus + right[0], step(True, -1))
    low = mine[:2] + right[1] + near
    high = mine[2:] + left[1] + far
    left = send(jnp.stack([high[0, 0], low[1, 1]]), step(False, 1))
    right = send(jnp.stack([high[0, 1], high[1, 0]]), step(False, -1))
    near = send(low[1, 0] + left[0], step(False, 1))
    far = send(high[1, 1] + right[0], step(False, -1))
    return jnp.stack([low[0, 0] + right[1] + near, low[0, 1] + left[1] + far])


def shards(activations, cotangent, master, moment, second):
    tr = lax.axis_index("tr")
    tokens = activations.shape[0]
    units = cotangent.shape[1] // 2
    away = lax.dynamic_slice_in_dim(cotangent, (1 - tr) * units, units, 1)
    own_keep = lax.dynamic_slice_in_dim(cotangent, tr * units, units, 1)
    own_came = send(away, PAIR)
    far_keep = send(own_keep, OTHER_CORE)
    ordered = feature_order(activations)
    half = ordered.shape[1] // 2
    far_act = send(ordered[:, half:], OTHER_CORE)
    both = jnp.stack([ordered[:, :half], far_act])
    gathered = []
    start = 0
    for rows in CHUNKS:
        size = rows * SIDE**2
        block = lax.all_gather(both[:, :, start : start + size], ("tc", "tr"), axis=0)
        gathered.append(block.reshape(4, 2, 2, tokens, size))
        start += size
    far_came = send(own_came, OTHER_CORE)
    cots = (own_keep, own_came, far_keep, far_came)
    sums = [summed(product(block, cots)) for block in gathered]
    rows = jnp.concatenate(sums, axis=1)
    rows = rows.reshape(2, 4, ROWS // 4, units).swapaxes(0, 1).reshape(8, ROWS // 4, units)
    rows = lax.all_to_all(rows, ("tc", "tr"), split_axis=0, concat_axis=0, tiled=True)
    grad = rows.swapaxes(0, 1).reshape(1, ROWS // 4, 8 * units)
    new_moment = first_decay * moment + (1.0 - first_decay) * grad
    new_second = second_decay * second + (1.0 - second_decay) * grad * grad
    update = new_moment / first_fix / (jnp.sqrt(new_second / second_fix) + epsilon)
    new_master = master - learn_rate * (update + weight_decay * master)
    return (new_master, new_moment, new_second)


def solution(mesh):
    state = P("tr", ("dp", "tc"), None)
    return jax.shard_map(
        shards,
        mesh=mesh,
        in_specs=(P(("dp", "tc"), "tr"), P(("dp", "tr"), "tc"), state, state, state),
        out_specs=(state, state, state),
        check_vma=False,
    )
```

```python
import jax
import jax.numpy as jnp
from jax import lax
from jax.experimental import pallas as pl
from jax.experimental.pallas import tpu as pltpu
from jax.sharding import PartitionSpec as P

first_decay = 0.9
second_decay = 0.95
learn_rate = 0.0003
weight_decay = 0.1
epsilon = 1e-08
first_fix = 1.0 - 0.9**10
second_fix = 1.0 - 0.95**10

AXES = ("dp", "tr", "tc")
SIDE = 4
ROWS = 48
CHUNKS = (24, 24)


def moves(where):
    pairs = []
    for dp in range(32):
        for tr in range(2):
            for tc in range(4):
                y, x, core, z = where(dp // 8, dp // 2 % 4, dp % 2, 2 * tc + tr)
                to = (y % 4 * 8 + x % 4 * 2 + core % 2, z % 2, z % 8 // 2)
                pairs.append(((dp * 2 + tr) * 4 + tc, (to[0] * 2 + to[1]) * 4 + to[2]))
    return pairs


def step(first, sign):
    def where(y, x, core, z):
        if (core == 0) == first:
            return y, x + sign, core, z
        return y + sign, x, core, z

    return moves(where)


def send(array, pairs):
    return lax.ppermute(array, AXES, pairs)


OTHER_CORE = moves(lambda y, x, core, z: (y, x, 1 - core, z))
PAIR = moves(lambda y, x, core, z: (y, x, core, z ^ 1))


def feature_order(activations):
    dp = lax.axis_index("dp")
    my_y, my_x, core = dp // 8, dp // 2 % 4, dp % 2
    column = lax.broadcasted_iota(jnp.int32, (1, 2 * SIDE * SIDE * ROWS), 1)
    half, rest = column // (SIDE * SIDE * ROWS), column % (SIDE * SIDE * ROWS)
    target = jnp.where(half == 0, core, 1 - core)
    source = jnp.zeros_like(column)
    start = 0
    for rows in CHUNKS:
        size = SIDE * SIDE * rows
        inside = rest - start * SIDE * SIDE
        near, far, row = inside // (SIDE * rows), inside // rows % SIDE, inside % rows
        x = jnp.where(target == 0, my_x + near, my_x + far) % SIDE
        y = jnp.where(target == 0, my_y + far, my_y + near) % SIDE
        feature = (y * SIDE + x) * 2 * ROWS + target * ROWS + start + row
        source = jnp.where((inside >= 0) & (inside < size), feature, source)
        start += rows
    feature = lax.broadcasted_iota(jnp.int32, (activations.shape[1], column.shape[1]), 0)
    chosen = (feature == source).astype(activations.dtype)
    return jnp.dot(activations, chosen, preferred_element_type=jnp.float32).astype(activations.dtype)


def product_kernel(act, own_keep, own_came, far_keep, far_came, plus, minus, add_plus, add_minus, mine):
    tr = lax.axis_index("tr")
    features = act.shape[-1]

    def part(half, replica, cot):
        rows = act[pl.ds(2 * half, 2), 0, replica].reshape(cot.shape[0], features)
        return lax.dot_general(rows, cot[...], (((0,), (0,)), ((), ())), preferred_element_type=jnp.float32)

    total = part(tr, 0, own_keep) + part(1 - tr, 0, own_came)
    total = total + (part(tr, 1, far_keep) + part(1 - tr, 1, far_came))
    total = total.reshape(SIDE, SIDE, 1, features // SIDE**2, total.shape[-1])
    plus[0] = total[2, :2]
    plus[1] = total[1, 2:]
    minus[0] = total[2, 2:]
    minus[1] = total[3, :2]
    add_plus[...] = total[1, :2]
    add_minus[...] = total[3, 2:]
    mine[...] = total[0]


def product(act, cots):
    features, units = act.shape[-1], cots[0].shape[1]
    rows = features // SIDE**2
    whole = pl.BlockSpec(cots[0].shape, lambda i: (0, 0))
    lead = pl.BlockSpec((2, 2, 1, rows, units), lambda i: (0, 0, i, 0, 0))
    pack = pl.BlockSpec((2, 2, 1, rows, units), lambda i: (0, 0, i, 0, 0))
    part = pl.BlockSpec((2, 1, rows, units), lambda i: (0, i, 0, 0))
    full = pl.BlockSpec((SIDE, 1, rows, units), lambda i: (0, i, 0, 0))
    packed = jax.ShapeDtypeStruct((2, 2, 2, rows, units), jnp.float32)
    parted = jax.ShapeDtypeStruct((2, 2, rows, units), jnp.float32)
    return pl.pallas_call(
        product_kernel,
        grid=(2,),
        in_specs=[pl.BlockSpec((4, 1, 2, act.shape[3], features), lambda i: (0, i, 0, 0, 0))] + [whole] * 4,
        out_specs=[lead, pack, part, part, full],
        out_shape=[packed, packed, parted, parted, jax.ShapeDtypeStruct((SIDE, 2, rows, units), jnp.float32)],
        compiler_params=pltpu.CompilerParams(vmem_limit_bytes=58 * 2**20),
        cost_estimate=pl.CostEstimate(
            flops=2 * 2 * features * 4 * cots[0].shape[0] * units, bytes_accessed=12 * 2**20, transcendentals=0
        ),
    )(act, *cots)


def summed(parts):
    plus, minus, add_plus, add_minus, mine = parts
    left = send(plus, step(True, 1))
    right = send(minus, step(True, -1))
    near = send(add_plus + left[0], step(True, 1))
    far = send(add_minus + right[0], step(True, -1))
    low = mine[:2] + right[1] + near
    high = mine[2:] + left[1] + far
    left = send(jnp.stack([high[0, 0], low[1, 1]]), step(False, 1))
    right = send(jnp.stack([high[0, 1], high[1, 0]]), step(False, -1))
    near = send(low[1, 0] + left[0], step(False, 1))
    far = send(high[1, 1] + right[0], step(False, -1))
    return jnp.stack([low[0, 0] + right[1] + near, low[0, 1] + left[1] + far])


def shards(activations, cotangent, master, moment, second):
    tr = lax.axis_index("tr")
    tokens = activations.shape[0]
    units = cotangent.shape[1] // 2
    away = lax.dynamic_slice_in_dim(cotangent, (1 - tr) * units, units, 1)
    own_keep = lax.dynamic_slice_in_dim(cotangent, tr * units, units, 1)
    own_came = send(away, PAIR)
    far_keep = send(own_keep, OTHER_CORE)
    ordered = feature_order(activations)
    half = ordered.shape[1] // 2
    far_act = send(ordered[:, half:], OTHER_CORE)
    both = jnp.stack([ordered[:, :half], far_act])
    gathered = []
    start = 0
    for rows in CHUNKS:
        size = rows * SIDE**2
        block = lax.all_gather(both[:, :, start : start + size], ("tc", "tr"), axis=0)
        gathered.append(block.reshape(4, 2, 2, tokens, size))
        start += size
    far_came = send(own_came, OTHER_CORE)
    cots = (own_keep, own_came, far_keep, far_came)
    sums = []
    for block in gathered:
        if sums:
            block, sums[-1] = lax.optimization_barrier((block, sums[-1]))
        sums.append(summed(product(block, cots)))
    rows = jnp.concatenate(sums, axis=1).reshape(2, 4, ROWS // 4, 8, units // 8)
    return updated(rows, master, moment, second)


def updated(rows, master, moment, second):
    tr, tc = lax.axis_index("tr"), lax.axis_index("tc")
    keep = lax.dynamic_index_in_dim(rows, tr, 0, keepdims=False)
    came = send(lax.dynamic_index_in_dim(rows, 1 - tr, 0, keepdims=False), PAIR)
    both = jnp.stack([keep, came], axis=1)
    pieces = []
    for k in range(4):
        piece = lax.dynamic_index_in_dim(both, (tc + k) % 4, 0, keepdims=False)
        pieces.append(send(piece, moves(lambda y, x, core, z: (y, x, core, z + 2 * k))) if k else piece)
    wide = (ROWS // 4, 8 * rows.shape[3], rows.shape[4])
    flat = [array.reshape(wide) for array in (master, moment, second)]
    outs = pl.pallas_call(
        update_kernel,
        out_shape=[jax.ShapeDtypeStruct(wide, jnp.float32)] * 3,
        compiler_params=pltpu.CompilerParams(vmem_limit_bytes=16 * 2**20),
    )(*pieces, *flat)
    return tuple(out.reshape(master.shape) for out in outs)


def update_kernel(piece_0, piece_1, piece_2, piece_3, master, moment, second, new_master, new_moment, new_second):
    tr, tc = lax.axis_index("tr"), lax.axis_index("tc")
    for k, piece in enumerate((piece_0, piece_1, piece_2, piece_3)):
        for came in range(2):
            owner = 2 * ((tc + 4 - k) % 4) + (1 - tr if came else tr)
            place = (slice(None), pl.ds(pl.multiple_of(owner * 8, 8), 8), slice(None))
            grad = piece[came]
            first = first_decay * moment[place] + (1.0 - first_decay) * grad
            square = second_decay * second[place] + (1.0 - second_decay) * grad * grad
            old = master[place]
            update = first / first_fix / (jnp.sqrt(square / second_fix) + epsilon)
            new_moment[place] = first
            new_second[place] = square
            new_master[place] = old - learn_rate * (update + weight_decay * old)


def solution(mesh):
    state = P("tr", ("dp", "tc"), None)
    return jax.shard_map(
        shards,
        mesh=mesh,
        in_specs=(P(("dp", "tc"), "tr"), P(("dp", "tr"), "tc"), state, state, state),
        out_specs=(state, state, state),
        check_vma=False,
    )
```

```python
import jax
import jax.numpy as jnp
from jax import lax
from jax.experimental import pallas as pl
from jax.experimental.pallas import tpu as pltpu
from jax.sharding import PartitionSpec as P

first_decay = 0.9
second_decay = 0.95
learn_rate = 0.0003
weight_decay = 0.1
epsilon = 1e-08
first_fix = 1.0 - 0.9**10
second_fix = 1.0 - 0.95**10

AXES = ("dp", "tr", "tc")
SIDE = 4
ROWS = 48
CHUNKS = (24, 24)


def moves(where):
    pairs = []
    for dp in range(32):
        for tr in range(2):
            for tc in range(4):
                y, x, core, z = where(dp // 8, dp // 2 % 4, dp % 2, 2 * tc + tr)
                to = (y % 4 * 8 + x % 4 * 2 + core % 2, z % 2, z % 8 // 2)
                pairs.append(((dp * 2 + tr) * 4 + tc, (to[0] * 2 + to[1]) * 4 + to[2]))
    return pairs


def step(first, hop):
    def where(y, x, core, z):
        if (core == 0) == first:
            return y, x + hop, core, z
        return y + hop, x, core, z

    return moves(where)


def send(array, pairs):
    return lax.ppermute(array, AXES, pairs)


OTHER_CORE = moves(lambda y, x, core, z: (y, x, 1 - core, z))
PAIR = moves(lambda y, x, core, z: (y, x, core, z ^ 1))


def feature_order(activations):
    dp = lax.axis_index("dp")
    my_y, my_x, core = dp // 8, dp // 2 % 4, dp % 2
    column = lax.broadcasted_iota(jnp.int32, (1, 2 * SIDE * SIDE * ROWS), 1)
    half, rest = column // (SIDE * SIDE * ROWS), column % (SIDE * SIDE * ROWS)
    target = jnp.where(half == 0, core, 1 - core)
    source = jnp.zeros_like(column)
    start = 0
    for rows in CHUNKS:
        size = SIDE * SIDE * rows
        inside = rest - start * SIDE * SIDE
        near, far, row = inside // (SIDE * rows), inside // rows % SIDE, inside % rows
        x = jnp.where(target == 0, my_x + near, my_x + far) % SIDE
        y = jnp.where(target == 0, my_y + far, my_y + near) % SIDE
        feature = (y * SIDE + x) * 2 * ROWS + target * ROWS + start + row
        source = jnp.where((inside >= 0) & (inside < size), feature, source)
        start += rows
    feature = lax.broadcasted_iota(jnp.int32, (activations.shape[1], column.shape[1]), 0)
    chosen = (feature == source).astype(activations.dtype)
    return jnp.dot(activations, chosen, preferred_element_type=jnp.float32).astype(activations.dtype)


def product_kernel(pieces, count, *refs):
    acts, cots = refs[:count], refs[count : count + 4]
    outs = refs[count + 4 : count + 8]
    act, cot, act_sem, cot_sem = refs[count + 8 :]
    tr, tc = lax.axis_index("tr"), lax.axis_index("tc")
    features = act.shape[-1]
    i = pl.program_id(0)

    @pl.when(i == 0)
    def fetch():
        copies = []
        for n, (piece, ref) in enumerate(zip(pieces, acts)):
            if piece is None:
                target = act
            else:
                z = (2 * tc + tr + 8 + piece[0]) % 8
                target = act.at[z // 2, z % 2]
                if piece[1] is not None:
                    target = target.at[piece[1]]
            copies.append(pltpu.make_async_copy(ref, target, act_sem.at[n]))
        late = [pltpu.make_async_copy(ref, cot.at[n], cot_sem.at[n]) for n, ref in enumerate(cots)]
        for copy in copies + late:
            copy.start()
        for copy in copies + late:
            copy.wait()

    def part(half, replica, n):
        rows = act[pl.ds(2 * half, 2), i, replica].reshape(cot.shape[1], features)
        return lax.dot_general(rows, cot[n], (((0,), (0,)), ((), ())), preferred_element_type=jnp.float32)

    total = part(tr, 0, 0) + part(1 - tr, 0, 1)
    total = total + (part(tr, 1, 2) + part(1 - tr, 1, 3))
    total = total.reshape(SIDE, SIDE, 1, features // SIDE**2, total.shape[-1])
    for near in range(SIDE):
        outs[near][...] = total[near]


def product(acts, pieces, cots):
    tokens, features = acts[0].shape[-2:]
    units = cots[0].shape[1]
    rows = features // SIDE**2
    return pl.pallas_call(
        lambda *refs: product_kernel(pieces, len(acts), *refs),
        grid=(2,),
        in_specs=[pl.BlockSpec(memory_space=pl.ANY)] * (len(acts) + 4),
        out_specs=[pl.BlockSpec((SIDE, 1, rows, units), lambda i: (0, i, 0, 0))] * SIDE,
        out_shape=[jax.ShapeDtypeStruct((SIDE, 2, rows, units), jnp.float32)] * SIDE,
        scratch_shapes=[
            pltpu.VMEM((4, 2, 2, tokens, features), acts[0].dtype),
            pltpu.VMEM((4,) + cots[0].shape, cots[0].dtype),
            pltpu.SemaphoreType.DMA((len(acts),)),
            pltpu.SemaphoreType.DMA((4,)),
        ],
        compiler_params=pltpu.CompilerParams(vmem_limit_bytes=58 * 2**20),
        cost_estimate=pl.CostEstimate(
            flops=2 * 2 * features * 4 * cots[0].shape[0] * units, bytes_accessed=12 * 2**20, transcendentals=0
        ),
    )(*acts, *cots)


def gathered_in_ring(own):
    up, down = moves(lambda y, x, core, z: (y, x, core, z + 1)), moves(lambda y, x, core, z: (y, x, core, z - 1))
    acts, pieces = [own], [(0, None)]
    below, above = own, own
    for hop in range(1, 4):
        below, above = send(below, up), send(above, down)
        acts += [below, above]
        pieces += [(-hop, None), (hop, None)]
    acts += [send(below[0], up), send(above[1], down)]
    pieces += [(4, 0), (4, 1)]
    return acts, pieces


def summed(parts):
    first = [send(parts[hop], step(True, hop)) for hop in (1, 3, 2)]
    far = [parts[0][s] + first[0][s] + (first[1][s] + first[2][s]) for s in range(SIDE)]
    second = [send(far[hop], step(False, hop)) for hop in (1, 3, 2)]
    return far[0] + second[0] + (second[1] + second[2])


def shards(activations, cotangent, master, moment, second):
    tr = lax.axis_index("tr")
    tokens = activations.shape[0]
    units = cotangent.shape[1] // 2
    away = lax.dynamic_slice_in_dim(cotangent, (1 - tr) * units, units, 1)
    own_keep = lax.dynamic_slice_in_dim(cotangent, tr * units, units, 1)
    own_came = send(away, PAIR)
    far_keep = send(own_keep, OTHER_CORE)
    ordered = feature_order(activations)
    half = ordered.shape[1] // 2
    far_act = send(ordered[:, half:], OTHER_CORE)
    both = jnp.stack([ordered[:, :half], far_act])
    size = CHUNKS[0] * SIDE**2
    whole = lax.all_gather(both[:, :, :size], ("tc", "tr"), axis=0)
    acts, pieces = gathered_in_ring(both[:, :, size:])
    far_came = send(own_came, OTHER_CORE)
    cots = (own_keep, own_came, far_keep, far_came)
    sums = [
        summed(product([whole.reshape(4, 2, 2, tokens, size)], [None], cots)),
        summed(product(acts, pieces, cots)),
    ]
    rows = jnp.concatenate(sums, axis=1).reshape(2, 4, ROWS // 4, 8, units // 8)
    return updated(rows, master, moment, second)


def updated(rows, master, moment, second):
    tr, tc = lax.axis_index("tr"), lax.axis_index("tc")
    keep = lax.dynamic_index_in_dim(rows, tr, 0, keepdims=False)
    came = send(lax.dynamic_index_in_dim(rows, 1 - tr, 0, keepdims=False), PAIR)
    both = jnp.stack([keep, came], axis=1)
    pieces = []
    for k in range(4):
        piece = lax.dynamic_index_in_dim(both, (tc + k) % 4, 0, keepdims=False)
        pieces.append(send(piece, moves(lambda y, x, core, z: (y, x, core, z + 2 * k))) if k else piece)
    wide = (ROWS // 4, 8 * rows.shape[3], rows.shape[4])
    flat = [array.reshape(wide) for array in (master, moment, second)]
    outs = pl.pallas_call(
        update_kernel,
        out_shape=[jax.ShapeDtypeStruct(wide, jnp.float32)] * 3,
        compiler_params=pltpu.CompilerParams(vmem_limit_bytes=16 * 2**20),
    )(*pieces, *flat)
    return tuple(out.reshape(master.shape) for out in outs)


def update_kernel(piece_0, piece_1, piece_2, piece_3, master, moment, second, new_master, new_moment, new_second):
    tr, tc = lax.axis_index("tr"), lax.axis_index("tc")
    for k, piece in enumerate((piece_0, piece_1, piece_2, piece_3)):
        for came in range(2):
            owner = 2 * ((tc + 4 - k) % 4) + (1 - tr if came else tr)
            place = (slice(None), pl.ds(pl.multiple_of(owner * 8, 8), 8), slice(None))
            grad = piece[came]
            first = first_decay * moment[place] + (1.0 - first_decay) * grad
            square = second_decay * second[place] + (1.0 - second_decay) * grad * grad
            old = master[place]
            update = first / first_fix / (jnp.sqrt(square / second_fix) + epsilon)
            new_moment[place] = first
            new_second[place] = square
            new_master[place] = old - learn_rate * (update + weight_decay * old)


def solution(mesh):
    state = P("tr", ("dp", "tc"), None)
    return jax.shard_map(
        shards,
        mesh=mesh,
        in_specs=(P(("dp", "tc"), "tr"), P(("dp", "tr"), "tc"), state, state, state),
        out_specs=(state, state, state),
        check_vma=False,
    )
```

```python
import jax
import jax.numpy as jnp
from jax import lax
from jax.experimental import pallas as pl
from jax.experimental.pallas import tpu as pltpu
from jax.sharding import PartitionSpec as P

first_decay = 0.9
second_decay = 0.95
learn_rate = 0.0003
weight_decay = 0.1
epsilon = 1e-08
first_fix = 1.0 - 0.9**10
second_fix = 1.0 - 0.95**10

AXES = ("dp", "tr", "tc")
SIDE = 4
ROWS = 48
CHUNKS = (32, 16)


def moves(where):
    pairs = []
    for dp in range(32):
        for tr in range(2):
            for tc in range(4):
                y, x, core, z = where(dp // 8, dp // 2 % 4, dp % 2, 2 * tc + tr)
                to = (y % 4 * 8 + x % 4 * 2 + core % 2, z % 2, z % 8 // 2)
                pairs.append(((dp * 2 + tr) * 4 + tc, (to[0] * 2 + to[1]) * 4 + to[2]))
    return pairs


def step(first, hop):
    def where(y, x, core, z):
        if (core == 0) == first:
            return y, x + hop, core, z
        return y + hop, x, core, z

    return moves(where)


def send(array, pairs):
    return lax.ppermute(array, AXES, pairs)


OTHER_CORE = moves(lambda y, x, core, z: (y, x, 1 - core, z))
PAIR = moves(lambda y, x, core, z: (y, x, core, z ^ 1))


def feature_order(activations):
    dp = lax.axis_index("dp")
    my_y, my_x, core = dp // 8, dp // 2 % 4, dp % 2
    column = lax.broadcasted_iota(jnp.int32, (1, 2 * SIDE * SIDE * ROWS), 1)
    half, rest = column // (SIDE * SIDE * ROWS), column % (SIDE * SIDE * ROWS)
    target = jnp.where(half == 0, core, 1 - core)
    source = jnp.zeros_like(column)
    start = 0
    for rows in CHUNKS:
        size = SIDE * SIDE * rows
        inside = rest - start * SIDE * SIDE
        near, far, row = inside // (SIDE * rows), inside // rows % SIDE, inside % rows
        x = jnp.where(target == 0, my_x + near, my_x + far) % SIDE
        y = jnp.where(target == 0, my_y + far, my_y + near) % SIDE
        feature = (y * SIDE + x) * 2 * ROWS + target * ROWS + start + row
        source = jnp.where((inside >= 0) & (inside < size), feature, source)
        start += rows
    feature = lax.broadcasted_iota(jnp.int32, (activations.shape[1], column.shape[1]), 0)
    chosen = (feature == source).astype(activations.dtype)
    return jnp.dot(activations, chosen, preferred_element_type=jnp.float32).astype(activations.dtype)


def product_kernel(pieces, count, *refs):
    acts, cots = refs[:count], refs[count : count + 4]
    plus, minus, add_plus, add_minus, mine = refs[count + 4 : count + 9]
    act, cot, act_sem, cot_sem = refs[count + 9 :]
    tr, tc = lax.axis_index("tr"), lax.axis_index("tc")
    features = act.shape[-1]
    i = pl.program_id(0)

    @pl.when(i == 0)
    def fetch():
        copies = []
        for n, (piece, ref) in enumerate(zip(pieces, acts)):
            if piece is None:
                target = act
            else:
                z = (2 * tc + tr + 8 + piece[0]) % 8
                target = act.at[z // 2, z % 2]
                if piece[1] is not None:
                    target = target.at[piece[1]]
            copies.append(pltpu.make_async_copy(ref, target, act_sem.at[n]))
        late = [pltpu.make_async_copy(ref, cot.at[n], cot_sem.at[n]) for n, ref in enumerate(cots)]
        for copy in copies + late:
            copy.start()
        for copy in copies:
            copy.wait()

    def part(half, replica, n):
        @pl.when(i == 0)
        def arrived():
            pltpu.make_async_copy(cots[n], cot.at[n], cot_sem.at[n]).wait()

        rows = act[pl.ds(2 * half, 2), i, replica].reshape(cot.shape[1], features)
        return lax.dot_general(rows, cot[n], (((0,), (0,)), ((), ())), preferred_element_type=jnp.float32)

    total = part(tr, 0, 0) + part(1 - tr, 0, 1)
    total = total + (part(tr, 1, 2) + part(1 - tr, 1, 3))
    total = total.reshape(SIDE, SIDE, 1, features // SIDE**2, total.shape[-1])
    plus[0] = total[2, :2]
    plus[1] = total[1, 2:]
    minus[0] = total[2, 2:]
    minus[1] = total[3, :2]
    add_plus[...] = total[1, :2]
    add_minus[...] = total[3, 2:]
    mine[...] = total[0]


def product(acts, pieces, cots):
    tokens, features = acts[0].shape[-2:]
    units = cots[0].shape[1]
    rows = features // SIDE**2
    pack = pl.BlockSpec((2, 2, 1, rows, units), lambda i: (0, 0, i, 0, 0))
    part = pl.BlockSpec((2, 1, rows, units), lambda i: (0, i, 0, 0))
    full = pl.BlockSpec((SIDE, 1, rows, units), lambda i: (0, i, 0, 0))
    packed = jax.ShapeDtypeStruct((2, 2, 2, rows, units), jnp.float32)
    parted = jax.ShapeDtypeStruct((2, 2, rows, units), jnp.float32)
    return pl.pallas_call(
        lambda *refs: product_kernel(pieces, len(acts), *refs),
        grid=(2,),
        in_specs=[pl.BlockSpec(memory_space=pl.ANY)] * (len(acts) + 4),
        out_specs=[pack, pack, part, part, full],
        out_shape=[packed, packed, parted, parted, jax.ShapeDtypeStruct((SIDE, 2, rows, units), jnp.float32)],
        scratch_shapes=[
            pltpu.VMEM((4, 2, 2, tokens, features), acts[0].dtype),
            pltpu.VMEM((4,) + cots[0].shape, cots[0].dtype),
            pltpu.SemaphoreType.DMA((len(acts),)),
            pltpu.SemaphoreType.DMA((4,)),
        ],
        compiler_params=pltpu.CompilerParams(vmem_limit_bytes=60 * 2**20),
        cost_estimate=pl.CostEstimate(
            flops=2 * 2 * features * 4 * cots[0].shape[0] * units, bytes_accessed=12 * 2**20, transcendentals=0
        ),
    )(*acts, *cots)


UP = moves(lambda y, x, core, z: (y, x, core, z + 1))
DOWN = moves(lambda y, x, core, z: (y, x, core, z - 1))


def ring(own):
    acts, pieces = [own], [(0, None)]
    below, above = own, own
    for hop in range(1, 4):
        below, above = send(below, UP), send(above, DOWN)
        acts += [below, above]
        pieces += [(-hop, None), (hop, None)]
    return acts, pieces


def ring_end(acts, pieces):
    return acts + [send(acts[-2][0], UP), send(acts[-1][1], DOWN)], pieces + [(4, 0), (4, 1)]


def summed(parts):
    plus, minus, add_plus, add_minus, mine = parts
    left = send(plus, step(True, 1))
    right = send(minus, step(True, -1))
    near = send(add_plus + left[0], step(True, 1))
    far = send(add_minus + right[0], step(True, -1))
    low = [mine[s] + right[1, s] + near[s] for s in range(2)]
    high = [mine[2 + s] + left[1, s] + far[s] for s in range(2)]
    came = [send(low[1], step(False, 1)), send(high[1], step(False, -1)), send(high[0], step(False, 2))]
    return low[0] + came[0] + (came[1] + came[2])


def shards(activations, cotangent, master, moment, second):
    tr = lax.axis_index("tr")
    tokens = activations.shape[0]
    units = cotangent.shape[1] // 2
    away = lax.dynamic_slice_in_dim(cotangent, (1 - tr) * units, units, 1)
    own_keep = lax.dynamic_slice_in_dim(cotangent, tr * units, units, 1)
    activations, away, own_keep = lax.optimization_barrier((activations, away, own_keep))
    own_came = send(away, PAIR)
    far_keep = send(own_keep, OTHER_CORE)
    ordered = feature_order(activations)
    half = ordered.shape[1] // 2
    far_act = send(ordered[:, half:], OTHER_CORE)
    both = jnp.stack([ordered[:, :half], far_act])
    size = CHUNKS[0] * SIDE**2
    whole = lax.all_gather(both[:, :, :size], ("tc", "tr"), axis=0)
    rest, own_came = lax.optimization_barrier((both[:, :, size:], own_came))
    acts, pieces = ring(rest)
    far_came = send(own_came, OTHER_CORE)
    cots = (own_keep, own_came, far_keep, far_came)
    parts = product([whole.reshape(4, 2, 2, tokens, size)], [None], cots)
    acts[-2:], parts = lax.optimization_barrier((acts[-2:], parts))
    acts, pieces = ring_end(acts, pieces)
    sums = [summed(parts), summed(product(acts, pieces, cots))]
    rows = jnp.concatenate(sums, axis=1).reshape(2, 4, ROWS // 4, 8, units // 8)
    return updated(rows, master, moment, second)


def updated(rows, master, moment, second):
    tr, tc = lax.axis_index("tr"), lax.axis_index("tc")
    keep = lax.dynamic_index_in_dim(rows, tr, 0, keepdims=False)
    came = send(lax.dynamic_index_in_dim(rows, 1 - tr, 0, keepdims=False), PAIR)
    both = jnp.stack([keep, came], axis=1)
    pieces = []
    for k in range(4):
        piece = lax.dynamic_index_in_dim(both, (tc + k) % 4, 0, keepdims=False)
        pieces.append(send(piece, moves(lambda y, x, core, z: (y, x, core, z + 2 * k))) if k else piece)
    wide = (ROWS // 4, 8 * rows.shape[3], rows.shape[4])
    flat = [array.reshape(wide) for array in (master, moment, second)]
    outs = pl.pallas_call(
        update_kernel,
        out_shape=[jax.ShapeDtypeStruct(wide, jnp.float32)] * 3,
        compiler_params=pltpu.CompilerParams(vmem_limit_bytes=16 * 2**20),
    )(*pieces, *flat)
    return tuple(out.reshape(master.shape) for out in outs)


def update_kernel(piece_0, piece_1, piece_2, piece_3, master, moment, second, new_master, new_moment, new_second):
    tr, tc = lax.axis_index("tr"), lax.axis_index("tc")
    for k, piece in enumerate((piece_0, piece_1, piece_2, piece_3)):
        for came in range(2):
            owner = 2 * ((tc + 4 - k) % 4) + (1 - tr if came else tr)
            place = (slice(None), pl.ds(pl.multiple_of(owner * 8, 8), 8), slice(None))
            grad = piece[came]
            first = first_decay * moment[place] + (1.0 - first_decay) * grad
            square = second_decay * second[place] + (1.0 - second_decay) * grad * grad
            old = master[place]
            update = first / first_fix / (jnp.sqrt(square / second_fix) + epsilon)
            new_moment[place] = first
            new_second[place] = square
            new_master[place] = old - learn_rate * (update + weight_decay * old)


def solution(mesh):
    state = P("tr", ("dp", "tc"), None)
    return jax.shard_map(
        shards,
        mesh=mesh,
        in_specs=(P(("dp", "tc"), "tr"), P(("dp", "tr"), "tc"), state, state, state),
        out_specs=(state, state, state),
        check_vma=False,
    )
```

```python
import jax
import jax.numpy as jnp
from jax import lax
from jax.experimental import pallas as pl
from jax.experimental.pallas import tpu as pltpu
from jax.sharding import PartitionSpec as P

first_decay = 0.9
second_decay = 0.95
learn_rate = 0.0003
weight_decay = 0.1
epsilon = 1e-08
first_fix = 1.0 - 0.9**10
second_fix = 1.0 - 0.95**10

AXES = ("dp", "tr", "tc")
SIDE = 4
ROWS = 48
CHUNKS = (24, 24)


def moves(where):
    pairs = []
    for dp in range(32):
        for tr in range(2):
            for tc in range(4):
                y, x, core, z = where(dp // 8, dp // 2 % 4, dp % 2, 2 * tc + tr)
                to = (y % 4 * 8 + x % 4 * 2 + core % 2, z % 2, z % 8 // 2)
                pairs.append(((dp * 2 + tr) * 4 + tc, (to[0] * 2 + to[1]) * 4 + to[2]))
    return pairs


def step(first, hop):
    def where(y, x, core, z):
        if (core == 0) == first:
            return y, x + hop, core, z
        return y + hop, x, core, z

    return moves(where)


def send(array, pairs):
    return lax.ppermute(array, AXES, pairs)


OTHER_CORE = moves(lambda y, x, core, z: (y, x, 1 - core, z))
PAIR = moves(lambda y, x, core, z: (y, x, core, z ^ 1))


def feature_order(activations):
    dp = lax.axis_index("dp")
    my_y, my_x, core = dp // 8, dp // 2 % 4, dp % 2
    column = lax.broadcasted_iota(jnp.int32, (1, 2 * SIDE * SIDE * ROWS), 1)
    half, rest = column // (SIDE * SIDE * ROWS), column % (SIDE * SIDE * ROWS)
    target = jnp.where(half == 0, core, 1 - core)
    source = jnp.zeros_like(column)
    start = 0
    for rows in CHUNKS:
        size = SIDE * SIDE * rows
        inside = rest - start * SIDE * SIDE
        near, far, row = inside // (SIDE * rows), inside // rows % SIDE, inside % rows
        x = jnp.where(target == 0, my_x + near, my_x + far) % SIDE
        y = jnp.where(target == 0, my_y + far, my_y + near) % SIDE
        feature = (y * SIDE + x) * 2 * ROWS + target * ROWS + start + row
        source = jnp.where((inside >= 0) & (inside < size), feature, source)
        start += rows
    feature = lax.broadcasted_iota(jnp.int32, (activations.shape[1], column.shape[1]), 0)
    chosen = (feature == source).astype(activations.dtype)
    ordered = lax.dot_general(chosen, activations, (((0,), (1,)), ((), ())), preferred_element_type=jnp.float32)
    return ordered.astype(activations.dtype)


def product_kernel(pieces, *refs):
    count = len(pieces)
    acts, cots = refs[:count], refs[count : count + 4]
    plus, minus, add_plus, add_minus, mine = refs[count + 4 : count + 9]
    act, cot, act_sem, cot_sem = refs[count + 9 :]
    tr, tc = lax.axis_index("tr"), lax.axis_index("tc")
    features = act.shape[1]
    tokens = act.shape[2] // 8
    i = pl.program_id(0)

    def place(n, ref, z, replica):
        start = pl.multiple_of(replica * 4 * tokens + z // 2 * tokens, tokens)
        return pltpu.make_async_copy(ref, act.at[z % 2, :, pl.ds(start, tokens)], act_sem.at[n])

    def copies_of(replica):
        copies = []
        for piece, ref in zip(pieces, acts):
            for n in range(8 if piece is None else 1):
                if piece is not None and piece[1] not in (None, replica):
                    continue
                if piece is None:
                    source, z = ref.at[n, replica], n
                else:
                    source = ref.at[replica] if piece[1] is None else ref
                    z = (2 * tc + tr + 8 + piece[0]) % 8
                copies.append(place(8 * replica + len(copies), source, z, replica))
        for came in range(2):
            half = 1 - tr if came else tr
            start = pl.multiple_of(replica * 4 * tokens + half * 2 * tokens, 2 * tokens)
            n = 2 * replica + came
            copies.append(pltpu.make_async_copy(cots[n], cot.at[pl.ds(start, 2 * tokens)], cot_sem.at[n]))
        return copies

    @pl.when(i == 0)
    def fetch():
        for copy in copies_of(0) + copies_of(1):
            copy.start()

    def part(replica):
        @pl.when(i == 0)
        def arrived():
            for copy in copies_of(replica):
                copy.wait()

        depth = slice(replica * 4 * tokens, (replica + 1) * 4 * tokens)
        return jnp.dot(act[i, :, depth], cot[depth], preferred_element_type=jnp.float32)

    total = part(0)
    total = total + part(1)
    total = total.reshape(SIDE, SIDE, 1, features // SIDE**2, total.shape[-1])
    plus[0] = total[2, :2]
    plus[1] = total[1, 2:]
    minus[0] = total[2, 2:]
    minus[1] = total[3, :2]
    add_plus[...] = total[1, :2]
    add_minus[...] = total[3, 2:]
    mine[...] = total[0]


def product(acts, pieces, cots):
    features, tokens = acts[0].shape[-2:]
    units = cots[0].shape[1]
    rows = features // SIDE**2
    pack = pl.BlockSpec((2, 2, 1, rows, units), lambda i: (0, 0, i, 0, 0))
    part = pl.BlockSpec((2, 1, rows, units), lambda i: (0, i, 0, 0))
    full = pl.BlockSpec((SIDE, 1, rows, units), lambda i: (0, i, 0, 0))
    packed = jax.ShapeDtypeStruct((2, 2, 2, rows, units), jnp.float32)
    parted = jax.ShapeDtypeStruct((2, 2, rows, units), jnp.float32)
    return pl.pallas_call(
        lambda *refs: product_kernel(pieces, *refs),
        grid=(2,),
        in_specs=[pl.BlockSpec(memory_space=pl.ANY)] * (len(acts) + 4),
        out_specs=[pack, pack, part, part, full],
        out_shape=[packed, packed, parted, parted, jax.ShapeDtypeStruct((SIDE, 2, rows, units), jnp.float32)],
        scratch_shapes=[
            pltpu.VMEM((2, features, 8 * tokens), acts[0].dtype),
            pltpu.VMEM((8 * tokens, units), cots[0].dtype),
            pltpu.SemaphoreType.DMA((16,)),
            pltpu.SemaphoreType.DMA((4,)),
        ],
        compiler_params=pltpu.CompilerParams(vmem_limit_bytes=60 * 2**20),
        cost_estimate=pl.CostEstimate(
            flops=2 * 2 * features * 8 * tokens * units, bytes_accessed=12 * 2**20, transcendentals=0
        ),
    )(*acts, *cots)


UP = moves(lambda y, x, core, z: (y, x, core, z + 1))
DOWN = moves(lambda y, x, core, z: (y, x, core, z - 1))


def ring(own):
    acts, pieces = [own], [(0, None)]
    below, above = own, own
    for hop in range(1, 4):
        below, above = send(below, UP), send(above, DOWN)
        acts += [below, above]
        pieces += [(-hop, None), (hop, None)]
    return acts, pieces


def ring_end(acts, pieces):
    return acts + [send(acts[-2][0], UP), send(acts[-1][1], DOWN)], pieces + [(4, 0), (4, 1)]


def summed(parts):
    plus, minus, add_plus, add_minus, mine = parts
    left = send(plus, step(True, 1))
    right = send(minus, step(True, -1))
    near = send(add_plus + left[0], step(True, 1))
    far = send(add_minus + right[0], step(True, -1))
    low = [mine[s] + right[1, s] + near[s] for s in range(2)]
    high = [mine[2 + s] + left[1, s] + far[s] for s in range(2)]
    came = [send(low[1], step(False, 1)), send(high[1], step(False, -1)), send(high[0], step(False, 2))]
    return low[0] + came[0] + (came[1] + came[2])


def shards(activations, cotangent, master, moment, second):
    tr = lax.axis_index("tr")
    units = cotangent.shape[1] // 2
    ordered = feature_order(activations)
    half = ordered.shape[0] // 2
    both = jnp.stack([ordered[:half], send(ordered[half:], OTHER_CORE)])
    away = lax.dynamic_slice_in_dim(cotangent, (1 - tr) * units, units, 1)
    own_keep = lax.dynamic_slice_in_dim(cotangent, tr * units, units, 1)
    own_came = send(away, PAIR)
    far_keep = send(own_keep, OTHER_CORE)
    size = CHUNKS[0] * SIDE**2
    whole = lax.all_gather(both[:, :size], ("tc", "tr"), axis=0)
    rest, own_came = lax.optimization_barrier((both[:, size:], own_came))
    acts, pieces = ring(rest)
    far_came = send(own_came, OTHER_CORE)
    cots = (own_keep, own_came, far_keep, far_came)
    parts = product([whole], [None], cots)
    acts[-2:], parts = lax.optimization_barrier((acts[-2:], parts))
    acts, pieces = ring_end(acts, pieces)
    sums = [summed(parts), summed(product(acts, pieces, cots))]
    rows = jnp.concatenate(sums, axis=1).reshape(2, 4, ROWS // 4, 8, units // 8)
    return updated(rows, master, moment, second)


def updated(rows, master, moment, second):
    tr, tc = lax.axis_index("tr"), lax.axis_index("tc")
    keep = lax.dynamic_index_in_dim(rows, tr, 0, keepdims=False)
    came = send(lax.dynamic_index_in_dim(rows, 1 - tr, 0, keepdims=False), PAIR)
    both = jnp.stack([keep, came], axis=1)
    pieces = []
    for k in range(4):
        piece = lax.dynamic_index_in_dim(both, (tc + k) % 4, 0, keepdims=False)
        pieces.append(send(piece, moves(lambda y, x, core, z: (y, x, core, z + 2 * k))) if k else piece)
    wide = (ROWS // 4, 8 * rows.shape[3], rows.shape[4])
    flat = [array.reshape(wide) for array in (master, moment, second)]
    outs = pl.pallas_call(
        update_kernel,
        out_shape=[jax.ShapeDtypeStruct(wide, jnp.float32)] * 3,
        compiler_params=pltpu.CompilerParams(vmem_limit_bytes=16 * 2**20),
    )(*pieces, *flat)
    return tuple(out.reshape(master.shape) for out in outs)


def update_kernel(piece_0, piece_1, piece_2, piece_3, master, moment, second, new_master, new_moment, new_second):
    tr, tc = lax.axis_index("tr"), lax.axis_index("tc")
    for k, piece in enumerate((piece_0, piece_1, piece_2, piece_3)):
        for came in range(2):
            owner = 2 * ((tc + 4 - k) % 4) + (1 - tr if came else tr)
            place = (slice(None), pl.ds(pl.multiple_of(owner * 8, 8), 8), slice(None))
            grad = piece[came]
            first = first_decay * moment[place] + (1.0 - first_decay) * grad
            square = second_decay * second[place] + (1.0 - second_decay) * grad * grad
            old = master[place]
            update = first / first_fix / (jnp.sqrt(square / second_fix) + epsilon)
            new_moment[place] = first
            new_second[place] = square
            new_master[place] = old - learn_rate * (update + weight_decay * old)


def solution(mesh):
    state = P("tr", ("dp", "tc"), None)
    return jax.shard_map(
        shards,
        mesh=mesh,
        in_specs=(P(("dp", "tc"), "tr"), P(("dp", "tr"), "tc"), state, state, state),
        out_specs=(state, state, state),
        check_vma=False,
    )
```

```python
import jax
import jax.numpy as jnp
from jax import lax
from jax.experimental import pallas as pl
from jax.experimental.pallas import tpu as pltpu
from jax.sharding import PartitionSpec as P

first_decay = 0.9
second_decay = 0.95
learn_rate = 0.0003
weight_decay = 0.1
epsilon = 1e-08
first_fix = 1.0 - 0.9**10
second_fix = 1.0 - 0.95**10

AXES = ("dp", "tr", "tc")
SIDE = 4
ROWS = 48
CHUNKS = (40, 8)


def moves(where):
    pairs = []
    for dp in range(32):
        for tr in range(2):
            for tc in range(4):
                y, x, core, z = where(dp // 8, dp // 2 % 4, dp % 2, 2 * tc + tr)
                to = (y % 4 * 8 + x % 4 * 2 + core % 2, z % 2, z % 8 // 2)
                pairs.append(((dp * 2 + tr) * 4 + tc, (to[0] * 2 + to[1]) * 4 + to[2]))
    return pairs


def step(first, hop):
    def where(y, x, core, z):
        if (core == 0) == first:
            return y, x + hop, core, z
        return y + hop, x, core, z

    return moves(where)


def send(array, pairs):
    return lax.ppermute(array, AXES, pairs)


OTHER_CORE = moves(lambda y, x, core, z: (y, x, 1 - core, z))
PAIR = moves(lambda y, x, core, z: (y, x, core, z ^ 1))


def feature_order(activations):
    dp = lax.axis_index("dp")
    my_y, my_x, core = dp // 8, dp // 2 % 4, dp % 2
    column = lax.broadcasted_iota(jnp.int32, (1, 2 * SIDE * SIDE * ROWS), 1)
    half, rest = column // (SIDE * SIDE * ROWS), column % (SIDE * SIDE * ROWS)
    target = jnp.where(half == 0, core, 1 - core)
    source = jnp.zeros_like(column)
    start = 0
    for rows in CHUNKS:
        size = SIDE * SIDE * rows
        inside = rest - start * SIDE * SIDE
        near, far, row = inside // (SIDE * rows), inside // rows % SIDE, inside % rows
        x = jnp.where(target == 0, my_x + near, my_x + far) % SIDE
        y = jnp.where(target == 0, my_y + far, my_y + near) % SIDE
        feature = (y * SIDE + x) * 2 * ROWS + target * ROWS + start + row
        source = jnp.where((inside >= 0) & (inside < size), feature, source)
        start += rows
    feature = lax.broadcasted_iota(jnp.int32, (activations.shape[1], column.shape[1]), 0)
    chosen = (feature == source).astype(activations.dtype)
    ordered = lax.dot_general(chosen, activations, (((0,), (1,)), ((), ())), preferred_element_type=jnp.float32)
    return ordered.astype(activations.dtype)


def product_kernel(gathered, *refs):
    cots = refs[:4]
    plus, minus, add_plus, add_minus, mine = refs[4:9]
    act, cot, act_sem, cot_sem = refs[9:]
    tr = lax.axis_index("tr")
    features = act.shape[1]
    tokens = act.shape[2] // 8
    i = pl.program_id(0)

    def copies_of(replica):
        copies = []
        for z in range(8):
            window = pl.ds((replica * 4 + z // 2) * tokens, tokens)
            copies.append(
                pltpu.make_async_copy(gathered.at[z, replica], act.at[z % 2, :, window], act_sem.at[8 * replica + z])
            )
        for came in range(2):
            half = 1 - tr if came else tr
            start = pl.multiple_of(replica * 4 * tokens + half * 2 * tokens, 2 * tokens)
            n = 2 * replica + came
            copies.append(pltpu.make_async_copy(cots[n], cot.at[pl.ds(start, 2 * tokens)], cot_sem.at[n]))
        return copies

    @pl.when(i == 0)
    def fetch():
        for copy in copies_of(0) + copies_of(1):
            copy.start()

    def part(replica):
        @pl.when(i == 0)
        def arrived():
            for copy in copies_of(replica):
                copy.wait()

        depth = slice(replica * 4 * tokens, (replica + 1) * 4 * tokens)
        return jnp.dot(act[i, :, depth], cot[depth], preferred_element_type=jnp.float32)

    total = part(0)
    total = total + part(1)
    total = total.reshape(SIDE, SIDE, 1, features // SIDE**2, total.shape[-1])
    plus[0] = total[2, :2]
    plus[1] = total[1, 2:]
    minus[0] = total[2, 2:]
    minus[1] = total[3, :2]
    add_plus[...] = total[1, :2]
    add_minus[...] = total[3, 2:]
    mine[...] = total[0]


def product(gathered, cots):
    features, tokens = gathered.shape[-2:]
    units = cots[0].shape[1]
    rows = features // SIDE**2
    pack = pl.BlockSpec((2, 2, 1, rows, units), lambda i: (0, 0, i, 0, 0))
    part = pl.BlockSpec((2, 1, rows, units), lambda i: (0, i, 0, 0))
    full = pl.BlockSpec((SIDE, 1, rows, units), lambda i: (0, i, 0, 0))
    packed = jax.ShapeDtypeStruct((2, 2, 2, rows, units), jnp.float32)
    parted = jax.ShapeDtypeStruct((2, 2, rows, units), jnp.float32)
    return pl.pallas_call(
        product_kernel,
        grid=(2,),
        in_specs=[pl.BlockSpec(memory_space=pl.ANY)] * 5,
        out_specs=[pack, pack, part, part, full],
        out_shape=[packed, packed, parted, parted, jax.ShapeDtypeStruct((SIDE, 2, rows, units), jnp.float32)],
        scratch_shapes=[
            pltpu.VMEM((2, features, 8 * tokens), gathered.dtype),
            pltpu.VMEM((8 * tokens, units), cots[0].dtype),
            pltpu.SemaphoreType.DMA((16,)),
            pltpu.SemaphoreType.DMA((4,)),
        ],
        compiler_params=pltpu.CompilerParams(vmem_limit_bytes=60 * 2**20),
        cost_estimate=pl.CostEstimate(
            flops=2 * 2 * features * 8 * tokens * units, bytes_accessed=12 * 2**20, transcendentals=0
        ),
    )(gathered, *cots)


def first_round(parts):
    plus, minus, add_plus, add_minus, mine = parts
    left = send(plus, step(True, 1))
    right = send(minus, step(True, -1))
    rest = mine[:2] + right[1], mine[2:] + left[1]
    return (add_plus + left[0], add_minus + right[0]), rest


def second_round(ready, rest):
    near = send(ready[0], step(True, 1))
    far = send(ready[1], step(True, -1))
    low = [rest[0][s] + near[s] for s in range(2)]
    high = [rest[1][s] + far[s] for s in range(2)]
    came = [send(low[1], step(False, 1)), send(high[1], step(False, -1)), send(high[0], step(False, 2))]
    return low[0] + came[0] + (came[1] + came[2])


def shards(activations, cotangent, master, moment, second):
    tr = lax.axis_index("tr")
    units = cotangent.shape[1] // 2
    ordered = feature_order(activations)
    half = ordered.shape[0] // 2
    both = jnp.stack([ordered[:half], send(ordered[half:], OTHER_CORE)])
    away = lax.dynamic_slice_in_dim(cotangent, (1 - tr) * units, units, 1)
    own_keep = lax.dynamic_slice_in_dim(cotangent, tr * units, units, 1)
    own_came = send(away, PAIR)
    far_keep = send(own_keep, OTHER_CORE)
    size = CHUNKS[0] * SIDE**2
    whole = lax.all_gather(both[:, :size], ("tc", "tr"), axis=0)
    last = lax.all_gather(both[:, size:], ("tc", "tr"), axis=0)
    far_came = send(own_came, OTHER_CORE)
    cots = (own_keep, own_came, far_keep, far_came)
    ready, rest = first_round(product(whole, cots))
    last, ready = lax.optimization_barrier((last, ready))
    sums = [second_round(ready, rest), second_round(*first_round(product(last, cots)))]
    rows = jnp.concatenate(sums, axis=1).reshape(2, 4, ROWS // 4, 8, units // 8)
    rows = rows.swapaxes(0, 1).reshape(8, ROWS // 4, 8, units // 8)
    rows = lax.all_to_all(rows, ("tc", "tr"), split_axis=0, concat_axis=0, tiled=True)
    return updated(rows, master, moment, second)


def updated(rows, master, moment, second):
    wide = (rows.shape[1], rows.shape[0] * rows.shape[2], rows.shape[3])
    flat = [array.reshape(wide) for array in (master, moment, second)]
    outs = pl.pallas_call(
        update_kernel,
        out_shape=[jax.ShapeDtypeStruct(wide, jnp.float32)] * 3,
        compiler_params=pltpu.CompilerParams(vmem_limit_bytes=16 * 2**20),
    )(rows, *flat)
    return tuple(out.reshape(master.shape) for out in outs)


def update_kernel(rows, master, moment, second, new_master, new_moment, new_second):
    for z in range(8):
        place = (slice(None), pl.ds(z * 8, 8), slice(None))
        grad = rows[z]
        first = first_decay * moment[place] + (1.0 - first_decay) * grad
        square = second_decay * second[place] + (1.0 - second_decay) * grad * grad
        old = master[place]
        update = first / first_fix / (jnp.sqrt(square / second_fix) + epsilon)
        new_moment[place] = first
        new_second[place] = square
        new_master[place] = old - learn_rate * (update + weight_decay * old)


def solution(mesh):
    state = P("tr", ("dp", "tc"), None)
    return jax.shard_map(
        shards,
        mesh=mesh,
        in_specs=(P(("dp", "tc"), "tr"), P(("dp", "tr"), "tc"), state, state, state),
        out_specs=(state, state, state),
        check_vma=False,
    )
```

```python
import jax
import jax.numpy as jnp
from jax import lax
from jax.experimental import pallas as pl
from jax.experimental.pallas import tpu as pltpu
from jax.sharding import PartitionSpec as P

first_decay = 0.9
second_decay = 0.95
learn_rate = 0.0003
weight_decay = 0.1
epsilon = 1e-08
first_fix = 1.0 - 0.9**10
second_fix = 1.0 - 0.95**10

AXES = ("dp", "tr", "tc")
SIDE = 4
ROWS = 48
GROUP = 4
QUARTER = 4 * ROWS


def moves(where):
    pairs = []
    for dp in range(32):
        for tr in range(2):
            for tc in range(4):
                y, x, core, z = where(dp // 8, dp // 2 % 4, dp % 2, 2 * tc + tr)
                to = (y % 4 * 8 + x % 4 * 2 + core % 2, z % 2, z % 8 // 2)
                pairs.append(((dp * 2 + tr) * 4 + tc, (to[0] * 2 + to[1]) * 4 + to[2]))
    return pairs


def onward(core):
    return 1 - 2 * core


def send(array, pairs):
    return lax.ppermute(array, AXES, pairs)


OTHER_CORE = moves(lambda y, x, core, z: (y, x, 1 - core, z))
PAIR = moves(lambda y, x, core, z: (y, x, core, z ^ 1))
MATE = [moves(lambda y, x, core, z: (y + 2 * (g // 2), x + 2 * (g % 2), core, z)) for g in range(GROUP)]
NEXT_X = moves(lambda y, x, core, z: (y, x + onward(core), core, z))
NEXT_Y = moves(lambda y, x, core, z: (y + onward(core), x, core, z))


def feature_order(activations):
    dp = lax.axis_index("dp")
    my_y, my_x, core = dp // 8, dp // 2 % 4, dp % 2
    column = lax.broadcasted_iota(jnp.int32, (1, 2 * GROUP * QUARTER), 1)
    row, block = column % ROWS, column // ROWS
    far_x, far_y, mate, half = block % 2, block // 2 % 2, block // 4 % GROUP, block // (4 * GROUP)
    target = jnp.where(half == 0, core, 1 - core)
    x = (my_x + 2 * (mate % 2) + far_x * onward(target) + SIDE) % SIDE
    y = (my_y + 2 * (mate // 2) + far_y * onward(target) + SIDE) % SIDE
    source = ((y * SIDE + x) * 2 + target) * ROWS + row
    feature = lax.broadcasted_iota(jnp.int32, (activations.shape[1], column.shape[1]), 0)
    chosen = (feature == source).astype(activations.dtype)
    ordered = lax.dot_general(chosen, activations, (((0,), (1,)), ((), ())), preferred_element_type=jnp.float32)
    return ordered.astype(activations.dtype)


def product_kernel(gathered, *refs):
    cots = refs[: 4 * GROUP]
    a_send, a_keep, b_send, b_keep = refs[4 * GROUP : 4 * GROUP + 4]
    act, cot, act_sem, cot_sem = refs[4 * GROUP + 4 :]
    tr = lax.axis_index("tr")
    replicas, quarter, tokens = gathered.shape[1:]
    depth = 4 * tokens

    def copies_of(replica):
        copies = []
        for z in range(8):
            window = pl.ds(replica * depth + z // 2 * tokens, tokens)
            target = act.at[pl.ds(z % 2 * quarter, quarter), window]
            copies.append(pltpu.make_async_copy(gathered.at[z, replica], target, act_sem.at[8 * replica + z]))
        for came in range(2):
            half = 1 - tr if came else tr
            start = pl.multiple_of(replica * depth + half * 2 * tokens, 2 * tokens)
            n = 2 * replica + came
            copies.append(pltpu.make_async_copy(cots[n], cot.at[pl.ds(start, 2 * tokens)], cot_sem.at[n]))
        return copies

    for replica in range(replicas):
        for copy in copies_of(replica):
            copy.start()
    total = None
    for replica in range(replicas):
        for copy in copies_of(replica):
            copy.wait()
        window = slice(replica * depth, (replica + 1) * depth)
        term = jnp.dot(act[:, window], cot[window], preferred_element_type=jnp.float32)
        total = term if total is None else total + term
    half = total.shape[1] // 2
    total = total.reshape(2, 2, 2, ROWS, 2 * half)
    for far in range(2):
        a_send[far] = total[:, far, 1, :, :half]
        a_keep[far] = total[:, far, 0, :, :half]
        b_send[far] = total[:, 1, far, :, half:]
        b_keep[far] = total[:, 0, far, :, half:]


def product(gathered, cots):
    replicas, quarter, tokens = gathered.shape[1:]
    units = cots[0].shape[1]
    part = jax.ShapeDtypeStruct((2, 2, ROWS, units // 2), jnp.float32)
    return pl.pallas_call(
        product_kernel,
        in_specs=[pl.BlockSpec(memory_space=pl.ANY)] * (1 + len(cots)),
        out_shape=[part] * 4,
        scratch_shapes=[
            pltpu.VMEM((2 * quarter, replicas * 4 * tokens), gathered.dtype),
            pltpu.VMEM((replicas * 4 * tokens, units), cots[0].dtype),
            pltpu.SemaphoreType.DMA((8 * replicas,)),
            pltpu.SemaphoreType.DMA((2 * replicas,)),
        ],
        compiler_params=pltpu.CompilerParams(vmem_limit_bytes=60 * 2**20),
        cost_estimate=pl.CostEstimate(
            flops=2 * 2 * quarter * replicas * 4 * tokens * units, bytes_accessed=28 * 2**20, transcendentals=0
        ),
    )(gathered, *cots)


def shards(activations, cotangent, master, moment, second):
    tr = lax.axis_index("tr")
    units = cotangent.shape[1] // 2
    ordered = feature_order(activations).reshape(2, GROUP, QUARTER, activations.shape[0])
    both = jnp.stack([ordered[0], send(ordered[1], OTHER_CORE)], axis=1)
    shared = jnp.stack([both[0]] + [send(both[g], MATE[g]) for g in (1, 2, 3)])
    away = lax.dynamic_slice_in_dim(cotangent, (1 - tr) * units, units, 1)
    own_keep = lax.dynamic_slice_in_dim(cotangent, tr * units, units, 1)
    own_came = send(away, PAIR)
    early, shared = lax.optimization_barrier((own_keep, shared))
    shared = shared.reshape(2 * GROUP, QUARTER, activations.shape[0])
    gathered = lax.all_gather(shared, ("tc", "tr"), axis=0)
    keep = [own_keep, send(early, MATE[1]), send(early, MATE[2])]
    keep.append(send(keep[1], MATE[2]))
    came = [own_came, send(own_came, MATE[1]), send(own_came, MATE[2])]
    came.append(send(came[2], MATE[1]))
    cots = []
    for g in range(GROUP):
        cots += [keep[g], came[g], send(keep[g], OTHER_CORE), send(came[g], OTHER_CORE)]
    a_send, a_keep, b_send, b_keep = product(gathered, cots)
    a_came, b_came = send(a_send, NEXT_X), send(b_send, NEXT_Y)
    a_last = send(a_keep[1] + a_came[1], NEXT_Y)
    b_last = send(b_keep[1] + b_came[1], NEXT_X)
    rows = jnp.concatenate([a_keep[0] + a_came[0] + a_last, b_keep[0] + b_came[0] + b_last], axis=2)
    rows = rows.reshape(2, 4, ROWS // 4, 8, units // 8)
    rows = rows.swapaxes(0, 1).reshape(8, ROWS // 4, 8, units // 8)
    rows = lax.all_to_all(rows, ("tc", "tr"), split_axis=0, concat_axis=0, tiled=True)
    return updated(rows, master, moment, second)


def updated(rows, master, moment, second):
    wide = (rows.shape[1], rows.shape[0] * rows.shape[2], rows.shape[3])
    flat = [array.reshape(wide) for array in (master, moment, second)]
    outs = pl.pallas_call(
        update_kernel,
        out_shape=[jax.ShapeDtypeStruct(wide, jnp.float32)] * 3,
        compiler_params=pltpu.CompilerParams(vmem_limit_bytes=16 * 2**20),
    )(rows, *flat)
    return tuple(out.reshape(master.shape) for out in outs)


def update_kernel(rows, master, moment, second, new_master, new_moment, new_second):
    for z in range(8):
        place = (slice(None), pl.ds(z * 8, 8), slice(None))
        grad = rows[z]
        first = first_decay * moment[place] + (1.0 - first_decay) * grad
        square = second_decay * second[place] + (1.0 - second_decay) * grad * grad
        old = master[place]
        update = first / first_fix / (jnp.sqrt(square / second_fix) + epsilon)
        new_moment[place] = first
        new_second[place] = square
        new_master[place] = old - learn_rate * (update + weight_decay * old)


def solution(mesh):
    state = P("tr", ("dp", "tc"), None)
    return jax.shard_map(
        shards,
        mesh=mesh,
        in_specs=(P(("dp", "tc"), "tr"), P(("dp", "tr"), "tc"), state, state, state),
        out_specs=(state, state, state),
        check_vma=False,
    )
```

```python
import jax
import jax.numpy as jnp
from jax import lax
from jax.experimental import pallas as pl
from jax.experimental.pallas import tpu as pltpu
from jax.sharding import PartitionSpec as P

first_decay = 0.9
second_decay = 0.95
learn_rate = 0.0003
weight_decay = 0.1
epsilon = 1e-08
first_fix = 1.0 - 0.9**10
second_fix = 1.0 - 0.95**10

AXES = ("dp", "tr", "tc")
SIDE = 4
ROWS = 48
GROUP = 4
QUARTER = 4 * ROWS


def moves(where):
    pairs = []
    for dp in range(32):
        for tr in range(2):
            for tc in range(4):
                y, x, core, z = where(dp // 8, dp // 2 % 4, dp % 2, 2 * tc + tr)
                to = (y % 4 * 8 + x % 4 * 2 + core % 2, z % 2, z % 8 // 2)
                pairs.append(((dp * 2 + tr) * 4 + tc, (to[0] * 2 + to[1]) * 4 + to[2]))
    return pairs


def onward(core):
    return 1 - 2 * core


def send(array, pairs):
    return lax.ppermute(array, AXES, pairs)


OTHER_CORE = moves(lambda y, x, core, z: (y, x, 1 - core, z))
PAIR = moves(lambda y, x, core, z: (y, x, core, z ^ 1))
MATE = [moves(lambda y, x, core, z: (y + 2 * (g // 2), x + 2 * (g % 2), core, z)) for g in range(GROUP)]
NEXT_X = moves(lambda y, x, core, z: (y, x + onward(core), core, z))
NEXT_Y = moves(lambda y, x, core, z: (y + onward(core), x, core, z))


def feature_order(activations):
    dp = lax.axis_index("dp")
    my_y, my_x, core = dp // 8, dp // 2 % 4, dp % 2
    column = lax.broadcasted_iota(jnp.int32, (1, 2 * GROUP * QUARTER), 1)
    row, block = column % ROWS, column // ROWS
    far_x, far_y, mate, half = block % 2, block // 2 % 2, block // 4 % GROUP, block // (4 * GROUP)
    target = jnp.where(half == 0, core, 1 - core)
    x = (my_x + 2 * (mate % 2) + far_x * onward(target) + SIDE) % SIDE
    y = (my_y + 2 * (mate // 2) + far_y * onward(target) + SIDE) % SIDE
    source = ((y * SIDE + x) * 2 + target) * ROWS + row
    feature = lax.broadcasted_iota(jnp.int32, (activations.shape[1], column.shape[1]), 0)
    chosen = (feature == source).astype(activations.dtype)
    ordered = lax.dot_general(chosen, activations, (((0,), (1,)), ((), ())), preferred_element_type=jnp.float32)
    return ordered.astype(activations.dtype)


def product_kernel(gathered, *refs):
    cots = refs[: 4 * GROUP]
    a_send, a_keep, b_send, b_keep = refs[4 * GROUP : 4 * GROUP + 4]
    act, cot, act_sem, cot_sem = refs[4 * GROUP + 4 :]
    tr = lax.axis_index("tr")
    replicas, quarter, tokens = gathered.shape[1:]
    depth = 4 * tokens

    def copies_of(replica):
        copies = []
        for z in range(8):
            window = pl.ds(replica * depth + z // 2 * tokens, tokens)
            target = act.at[pl.ds(z % 2 * quarter, quarter), window]
            copies.append(pltpu.make_async_copy(gathered.at[z, replica], target, act_sem.at[8 * replica + z]))
        for came in range(2):
            half = 1 - tr if came else tr
            start = pl.multiple_of(replica * depth + half * 2 * tokens, 2 * tokens)
            n = 2 * replica + came
            copies.append(pltpu.make_async_copy(cots[n], cot.at[pl.ds(start, 2 * tokens)], cot_sem.at[n]))
        return copies

    for replica in range(replicas):
        for copy in copies_of(replica):
            copy.start()
    total = None
    for replica in range(replicas):
        for copy in copies_of(replica):
            copy.wait()
        window = slice(replica * depth, (replica + 1) * depth)
        term = jnp.dot(act[:, window], cot[window], preferred_element_type=jnp.float32)
        total = term if total is None else total + term
    half = total.shape[1] // 2
    total = total.reshape(2, 2, 2, ROWS, 2 * half)
    for far in range(2):
        a_send[far] = total[:, far, 1, :, :half]
        a_keep[far] = total[:, far, 0, :, :half]
        b_send[far] = total[:, 1, far, :, half:]
        b_keep[far] = total[:, 0, far, :, half:]


def product(gathered, cots):
    replicas, quarter, tokens = gathered.shape[1:]
    units = cots[0].shape[1]
    part = jax.ShapeDtypeStruct((2, 2, ROWS, units // 2), jnp.float32)
    return pl.pallas_call(
        product_kernel,
        in_specs=[pl.BlockSpec(memory_space=pl.ANY)] * (1 + len(cots)),
        out_shape=[part] * 4,
        scratch_shapes=[
            pltpu.VMEM((2 * quarter, replicas * 4 * tokens), gathered.dtype),
            pltpu.VMEM((replicas * 4 * tokens, units), cots[0].dtype),
            pltpu.SemaphoreType.DMA((8 * replicas,)),
            pltpu.SemaphoreType.DMA((2 * replicas,)),
        ],
        compiler_params=pltpu.CompilerParams(vmem_limit_bytes=60 * 2**20),
        cost_estimate=pl.CostEstimate(
            flops=2 * 2 * quarter * replicas * 4 * tokens * units, bytes_accessed=28 * 2**20, transcendentals=0
        ),
    )(gathered, *cots)


def shards(activations, cotangent, master, moment, second):
    tr = lax.axis_index("tr")
    units = cotangent.shape[1] // 2
    ordered = feature_order(activations).reshape(2, GROUP, QUARTER, activations.shape[0])
    other = send(ordered[1], OTHER_CORE)
    tokens = cotangent.shape[0]
    away = [
        lax.dynamic_slice(cotangent, (start, (1 - tr) * units), (size, units))
        for start, size in ((0, tokens * 5 // 8), (tokens * 5 // 8, tokens * 3 // 8))
    ]
    own_keep = lax.dynamic_slice_in_dim(cotangent, tr * units, units, 1)
    other, away, own_keep = lax.optimization_barrier((other, away, own_keep))
    first_came, last_came = send(away[0], PAIR), send(away[1], PAIR)
    both = jnp.stack([ordered[0], other], axis=1)
    shared = jnp.stack([both[0]] + [send(both[g], MATE[g]) for g in (1, 2, 3)])
    far_keep = send(own_keep, OTHER_CORE)
    early, shared, first_came, far_keep = lax.optimization_barrier((own_keep, shared, first_came, far_keep))
    shared = shared.reshape(2 * GROUP, QUARTER, activations.shape[0])
    gathered = lax.all_gather(shared, ("tc", "tr"), axis=0)
    keep = [own_keep, send(early, MATE[1]), send(early, MATE[2])]
    came = [(first_came, last_came)] + [[send(part, MATE[g]) for part in (first_came, last_came)] for g in (1, 2)]
    came = lax.optimization_barrier([jnp.concatenate(parts) for parts in came])
    keep[1:] = lax.optimization_barrier(keep[1:])
    keep.append(send(keep[1], MATE[2]))
    came.append(send(came[2], MATE[1]))
    cots = []
    for g in range(GROUP):
        cots += [keep[g], came[g], send(keep[g], OTHER_CORE) if g else far_keep, send(came[g], OTHER_CORE)]
    a_send, a_keep, b_send, b_keep = product(gathered, cots)
    a_came, b_came = send(a_send, NEXT_X), send(b_send, NEXT_Y)
    a_last = send(a_keep[1] + a_came[1], NEXT_Y)
    b_last = send(b_keep[1] + b_came[1], NEXT_X)
    rows = jnp.concatenate([a_keep[0] + a_came[0] + a_last, b_keep[0] + b_came[0] + b_last], axis=2)
    rows = rows.reshape(2, 4, ROWS // 4, 8, units // 8)
    rows = rows.swapaxes(0, 1).reshape(8, ROWS // 4, 8, units // 8)
    rows = lax.all_to_all(rows, ("tc", "tr"), split_axis=0, concat_axis=0, tiled=True)
    return updated(rows, master, moment, second)


def updated(rows, master, moment, second):
    wide = (rows.shape[1], rows.shape[0] * rows.shape[2], rows.shape[3])
    flat = [array.reshape(wide) for array in (master, moment, second)]
    outs = pl.pallas_call(
        update_kernel,
        out_shape=[jax.ShapeDtypeStruct(wide, jnp.float32)] * 3,
        compiler_params=pltpu.CompilerParams(vmem_limit_bytes=16 * 2**20),
    )(rows, *flat)
    return tuple(out.reshape(master.shape) for out in outs)


def update_kernel(rows, master, moment, second, new_master, new_moment, new_second):
    for z in range(8):
        place = (slice(None), pl.ds(z * 8, 8), slice(None))
        grad = rows[z]
        first = first_decay * moment[place] + (1.0 - first_decay) * grad
        square = second_decay * second[place] + (1.0 - second_decay) * grad * grad
        old = master[place]
        update = first / first_fix / (jnp.sqrt(square / second_fix) + epsilon)
        new_moment[place] = first
        new_second[place] = square
        new_master[place] = old - learn_rate * (update + weight_decay * old)


def solution(mesh):
    state = P("tr", ("dp", "tc"), None)
    return jax.shard_map(
        shards,
        mesh=mesh,
        in_specs=(P(("dp", "tc"), "tr"), P(("dp", "tr"), "tc"), state, state, state),
        out_specs=(state, state, state),
        check_vma=False,
    )
```

```python
import jax
import jax.numpy as jnp
from jax import lax
from jax.experimental import pallas as pl
from jax.experimental.pallas import tpu as pltpu
from jax.sharding import PartitionSpec as P

first_decay = 0.9
second_decay = 0.95
learn_rate = 0.0003
weight_decay = 0.1
epsilon = 1e-08
first_fix = 1.0 - 0.9**10
second_fix = 1.0 - 0.95**10

AXES = ("dp", "tr", "tc")
SIDE = 4
ROWS = 48
GROUP = 4
SOURCES = ((0, 0), (1, 0), (-1, 0), (0, 1))
OWNERS = ((0, 0), (2, 1), (0, 2), (2, 3))
QUARTER = 4 * ROWS


def moves(where):
    pairs = []
    for dp in range(32):
        for tr in range(2):
            for tc in range(4):
                y, x, core, z = where(dp // 8, dp // 2 % 4, dp % 2, 2 * tc + tr)
                to = (y % 4 * 8 + x % 4 * 2 + core % 2, z % 2, z % 8 // 2)
                pairs.append(((dp * 2 + tr) * 4 + tc, (to[0] * 2 + to[1]) * 4 + to[2]))
    return pairs


def send(array, pairs):
    return lax.ppermute(array, AXES, pairs)


OTHER_CORE = moves(lambda y, x, core, z: (y, x, 1 - core, z))
PAIR = moves(lambda y, x, core, z: (y, x, core, z ^ 1))
FEED = [moves(lambda y, x, core, z: (y - dy, x - dx, core, z)) for dx, dy in SOURCES]
REDUCE = [moves(lambda y, x, core, z: (y + dy, x + dx, core, z)) for dx, dy in OWNERS]


def feature_order(activations):
    dp = lax.axis_index("dp")
    my_y, my_x, core = dp // 8, dp // 2 % 4, dp % 2
    column = lax.broadcasted_iota(jnp.int32, (1, 2 * GROUP * QUARTER), 1)
    row, block = column % ROWS, column // ROWS
    owner, feed, half = block % 4, block // 4 % GROUP, block // (4 * GROUP)
    target = jnp.where(half == 0, core, 1 - core)
    x, y = my_x, my_y
    for index in range(4):
        x = x + jnp.where(owner == index, OWNERS[index][0], 0) - jnp.where(feed == index, SOURCES[index][0], 0)
        y = y + jnp.where(owner == index, OWNERS[index][1], 0) - jnp.where(feed == index, SOURCES[index][1], 0)
    source = (((y + SIDE) % SIDE * SIDE + (x + SIDE) % SIDE) * 2 + target) * ROWS + row
    feature = lax.broadcasted_iota(jnp.int32, (activations.shape[1], column.shape[1]), 0)
    chosen = (feature == source).astype(activations.dtype)
    ordered = lax.dot_general(chosen, activations, (((0,), (1,)), ((), ())), preferred_element_type=jnp.float32)
    return ordered.astype(activations.dtype)


def product_kernel(gathered, *refs):
    cots = refs[: 4 * GROUP]
    outs = refs[4 * GROUP : 4 * GROUP + 4]
    act, cot, act_sem, cot_sem = refs[4 * GROUP + 4 :]
    tr = lax.axis_index("tr")
    replicas, quarter, tokens = gathered.shape[1:]
    depth = 4 * tokens

    def copies_of(replica):
        copies = []
        for z in range(8):
            window = pl.ds(replica * depth + z // 2 * tokens, tokens)
            target = act.at[pl.ds(z % 2 * quarter, quarter), window]
            copies.append(pltpu.make_async_copy(gathered.at[z, replica], target, act_sem.at[8 * replica + z]))
        for came in range(2):
            half = 1 - tr if came else tr
            start = pl.multiple_of(replica * depth + half * 2 * tokens, 2 * tokens)
            n = 2 * replica + came
            copies.append(pltpu.make_async_copy(cots[n], cot.at[pl.ds(start, 2 * tokens)], cot_sem.at[n]))
        return copies

    for replica in range(replicas):
        for copy in copies_of(replica):
            copy.start()
    total = None
    for replica in range(replicas):
        for copy in copies_of(replica):
            copy.wait()
        window = slice(replica * depth, (replica + 1) * depth)
        term = jnp.dot(act[:, window], cot[window], preferred_element_type=jnp.float32)
        total = term if total is None else total + term
    total = total.reshape(2, 4, ROWS, total.shape[1])
    for owner in range(4):
        outs[owner][...] = total[:, owner]


def product(gathered, cots):
    replicas, quarter, tokens = gathered.shape[1:]
    units = cots[0].shape[1]
    part = jax.ShapeDtypeStruct((2, ROWS, units), jnp.float32)
    return pl.pallas_call(
        product_kernel,
        in_specs=[pl.BlockSpec(memory_space=pl.ANY)] * (1 + len(cots)),
        out_shape=[part] * 4,
        scratch_shapes=[
            pltpu.VMEM((2 * quarter, replicas * 4 * tokens), gathered.dtype),
            pltpu.VMEM((replicas * 4 * tokens, units), cots[0].dtype),
            pltpu.SemaphoreType.DMA((8 * replicas,)),
            pltpu.SemaphoreType.DMA((2 * replicas,)),
        ],
        compiler_params=pltpu.CompilerParams(vmem_limit_bytes=60 * 2**20),
        cost_estimate=pl.CostEstimate(
            flops=2 * 2 * quarter * replicas * 4 * tokens * units, bytes_accessed=28 * 2**20, transcendentals=0
        ),
    )(gathered, *cots)


def shards(activations, cotangent, master, moment, second):
    tr = lax.axis_index("tr")
    units = cotangent.shape[1] // 2
    ordered = feature_order(activations).reshape(2, GROUP, QUARTER, activations.shape[0])
    other = send(ordered[1], OTHER_CORE)
    tokens = cotangent.shape[0]
    away = [
        lax.dynamic_slice(cotangent, (start, (1 - tr) * units), (size, units))
        for start, size in ((0, tokens * 5 // 8), (tokens * 5 // 8, tokens * 3 // 8))
    ]
    own_keep = lax.dynamic_slice_in_dim(cotangent, tr * units, units, 1)
    other, away, own_keep = lax.optimization_barrier((other, away, own_keep))
    first_came, last_came = send(away[0], PAIR), send(away[1], PAIR)
    both = jnp.stack([ordered[0], other], axis=1)
    shared = jnp.stack([both[0]] + [send(both[g], FEED[g]) for g in (1, 2, 3)])
    far_keep = send(own_keep, OTHER_CORE)
    early, shared, first_came, far_keep = lax.optimization_barrier((own_keep, shared, first_came, far_keep))
    shared = shared.reshape(2 * GROUP, QUARTER, activations.shape[0])
    gathered = lax.all_gather(shared, ("tc", "tr"), axis=0)
    own_came = jnp.concatenate([first_came, last_came])
    keep = [own_keep] + [send(early, FEED[g]) for g in (1, 2, 3)]
    came = [own_came] + [send(own_came, FEED[g]) for g in (1, 2, 3)]
    cots = []
    for g in range(GROUP):
        cots += [keep[g], came[g], send(keep[g], OTHER_CORE) if g else far_keep, send(came[g], OTHER_CORE)]
    parts = product(gathered, cots)
    far = [send(parts[owner], REDUCE[owner]) for owner in (1, 2, 3)]
    rows = parts[0] + far[0] + (far[1] + far[2])
    rows = rows.reshape(2, 4, ROWS // 4, 8, units // 8)
    rows = rows.swapaxes(0, 1).reshape(8, ROWS // 4, 8, units // 8)
    rows = lax.all_to_all(rows, ("tc", "tr"), split_axis=0, concat_axis=0, tiled=True)
    return updated(rows, master, moment, second)


def updated(rows, master, moment, second):
    wide = (rows.shape[1], rows.shape[0] * rows.shape[2], rows.shape[3])
    flat = [array.reshape(wide) for array in (master, moment, second)]
    outs = pl.pallas_call(
        update_kernel,
        out_shape=[jax.ShapeDtypeStruct(wide, jnp.float32)] * 3,
        compiler_params=pltpu.CompilerParams(vmem_limit_bytes=16 * 2**20),
    )(rows, *flat)
    return tuple(out.reshape(master.shape) for out in outs)


def update_kernel(rows, master, moment, second, new_master, new_moment, new_second):
    for z in range(8):
        place = (slice(None), pl.ds(z * 8, 8), slice(None))
        grad = rows[z]
        first = first_decay * moment[place] + (1.0 - first_decay) * grad
        square = second_decay * second[place] + (1.0 - second_decay) * grad * grad
        old = master[place]
        update = first / first_fix / (jnp.sqrt(square / second_fix) + epsilon)
        new_moment[place] = first
        new_second[place] = square
        new_master[place] = old - learn_rate * (update + weight_decay * old)


def solution(mesh):
    state = P("tr", ("dp", "tc"), None)
    return jax.shard_map(
        shards,
        mesh=mesh,
        in_specs=(P(("dp", "tc"), "tr"), P(("dp", "tr"), "tc"), state, state, state),
        out_specs=(state, state, state),
        check_vma=False,
    )
```

```python
import jax
import jax.numpy as jnp
from jax import lax
from jax.experimental import pallas as pl
from jax.experimental.pallas import tpu as pltpu
from jax.sharding import PartitionSpec as P

first_decay = 0.9
second_decay = 0.95
learn_rate = 0.0003
weight_decay = 0.1
epsilon = 1e-08
first_fix = 1.0 - 0.9**10
second_fix = 1.0 - 0.95**10

AXES = ("dp", "tr", "tc")
SIDE = 4
ROWS = 48
GROUP = 4
AHEAD = 3
SOURCES = ((0, 0), (1, 0), (-1, 0), (0, 1))
OWNERS = ((0, 0), (2, 1), (0, 2), (2, 3))
QUARTER = 4 * ROWS


def moves(where):
    pairs = []
    for dp in range(32):
        for tr in range(2):
            for tc in range(4):
                y, x, core, z = where(dp // 8, dp // 2 % 4, dp % 2, 2 * tc + tr)
                to = (y % 4 * 8 + x % 4 * 2 + core % 2, z % 2, z % 8 // 2)
                pairs.append(((dp * 2 + tr) * 4 + tc, (to[0] * 2 + to[1]) * 4 + to[2]))
    return pairs


def send(array, pairs):
    return lax.ppermute(array, AXES, pairs)


OTHER_CORE = moves(lambda y, x, core, z: (y, x, 1 - core, z))
PAIR = moves(lambda y, x, core, z: (y, x, core, z ^ 1))
FEED = [moves(lambda y, x, core, z: (y - dy, x - dx, core, z)) for dx, dy in SOURCES]
REDUCE = [moves(lambda y, x, core, z: (y + dy, x + dx, core, z)) for dx, dy in OWNERS]


def feature_order(activations):
    dp = lax.axis_index("dp")
    my_y, my_x, core = dp // 8, dp // 2 % 4, dp % 2
    column = lax.broadcasted_iota(jnp.int32, (1, 2 * GROUP * QUARTER), 1)
    row, block = column % ROWS, column // ROWS
    owner, feed, half = block % 4, block // 4 % GROUP, block // (4 * GROUP)
    target = jnp.where(half == 0, core, 1 - core)
    x, y = my_x, my_y
    for index in range(4):
        x = x + jnp.where(owner == index, OWNERS[index][0], 0) - jnp.where(feed == index, SOURCES[index][0], 0)
        y = y + jnp.where(owner == index, OWNERS[index][1], 0) - jnp.where(feed == index, SOURCES[index][1], 0)
    source = (((y + SIDE) % SIDE * SIDE + (x + SIDE) % SIDE) * 2 + target) * ROWS + row
    feature = lax.broadcasted_iota(jnp.int32, (activations.shape[1], column.shape[1]), 0)
    chosen = (feature == source).astype(activations.dtype)
    ordered = lax.dot_general(chosen, activations, (((0,), (1,)), ((), ())), preferred_element_type=jnp.float32)
    return ordered.astype(activations.dtype)


def product_kernel(gathered, *refs):
    cots = refs[: 4 * GROUP]
    outs = refs[4 * GROUP : 4 * GROUP + 4]
    act, cot, act_sem, cot_sem = refs[4 * GROUP + 4 :]
    tr = lax.axis_index("tr")
    replicas, quarter, tokens = gathered.shape[1:]
    depth = 4 * tokens

    def copies_of(replica):
        copies = []
        for z in range(8):
            window = pl.ds(replica * depth + z // 2 * tokens, tokens)
            target = act.at[pl.ds(z % 2 * quarter, quarter), window]
            copies.append(pltpu.make_async_copy(gathered.at[z, replica], target, act_sem.at[8 * replica + z]))
        for came in range(2):
            half = 1 - tr if came else tr
            start = pl.multiple_of(replica * depth + half * 2 * tokens, 2 * tokens)
            n = 2 * replica + came
            copies.append(pltpu.make_async_copy(cots[n], cot.at[pl.ds(start, 2 * tokens)], cot_sem.at[n]))
        return copies

    def fetch(replica):
        for copy in copies_of(replica):
            copy.start()

    for replica in range(AHEAD):
        fetch(replica)
    total = None
    for replica in range(replicas):
        if replica + AHEAD < replicas:
            fetch(replica + AHEAD)
        for copy in copies_of(replica):
            copy.wait()
        window = slice(replica * depth, (replica + 1) * depth)
        term = jnp.dot(act[:, window], cot[window], preferred_element_type=jnp.float32)
        total = term if total is None else total + term
    total = total.reshape(2, 4, ROWS, total.shape[1])
    for owner in range(4):
        outs[owner][...] = total[:, owner]


def product(gathered, cots):
    replicas, quarter, tokens = gathered.shape[1:]
    units = cots[0].shape[1]
    part = jax.ShapeDtypeStruct((2, ROWS, units), jnp.float32)
    return pl.pallas_call(
        product_kernel,
        in_specs=[pl.BlockSpec(memory_space=pl.ANY)] * (1 + len(cots)),
        out_shape=[part] * 4,
        scratch_shapes=[
            pltpu.VMEM((2 * quarter, replicas * 4 * tokens), gathered.dtype),
            pltpu.VMEM((replicas * 4 * tokens, units), cots[0].dtype),
            pltpu.SemaphoreType.DMA((8 * replicas,)),
            pltpu.SemaphoreType.DMA((2 * replicas,)),
        ],
        compiler_params=pltpu.CompilerParams(vmem_limit_bytes=60 * 2**20),
        cost_estimate=pl.CostEstimate(
            flops=2 * 2 * quarter * replicas * 4 * tokens * units, bytes_accessed=28 * 2**20, transcendentals=0
        ),
    )(gathered, *cots)


def shards(activations, cotangent, master, moment, second):
    tr = lax.axis_index("tr")
    units = cotangent.shape[1] // 2
    ordered = feature_order(activations).reshape(2, GROUP, QUARTER, activations.shape[0])
    other = send(ordered[1], OTHER_CORE)
    tokens = cotangent.shape[0]
    away = [
        lax.dynamic_slice(cotangent, (start, (1 - tr) * units), (size, units))
        for start, size in ((0, tokens // 2), (tokens // 2, tokens // 2))
    ]
    own_keep = lax.dynamic_slice_in_dim(cotangent, tr * units, units, 1)
    other, away, own_keep = lax.optimization_barrier((other, away, own_keep))
    first_came, last_came = send(away[0], PAIR), send(away[1], PAIR)
    both = jnp.stack([ordered[0], other], axis=1)
    shared = jnp.stack([both[0]] + [send(both[g], FEED[g]) for g in (1, 2, 3)])
    early, shared, first_came = lax.optimization_barrier((own_keep, shared, first_came))
    shared = shared.reshape(2 * GROUP, QUARTER, activations.shape[0])
    gathered = lax.all_gather(shared, ("tc", "tr"), axis=0)
    own_came = jnp.concatenate([first_came, last_came])
    keep = [own_keep] + [send(early, FEED[g]) for g in (1, 2, 3)]
    came = [own_came] + [send(own_came, FEED[g]) for g in (1, 2, 3)]
    cots = []
    for g in range(GROUP):
        cots += [keep[g], came[g], send(keep[g], OTHER_CORE), send(came[g], OTHER_CORE)]
    parts = product(gathered, cots)
    far = [send(parts[owner], REDUCE[owner]) for owner in (1, 3)]
    far.append(send(parts[2], REDUCE[2]))
    rows = parts[0] + far[0] + (far[1] + far[2])
    rows = rows.reshape(2, 4, ROWS // 4, 8, units // 8)
    rows = rows.swapaxes(0, 1).reshape(8, ROWS // 4, 8, units // 8)
    rows = lax.all_to_all(rows, ("tc", "tr"), split_axis=0, concat_axis=0, tiled=True)
    return updated(rows, master, moment, second)


def updated(rows, master, moment, second):
    wide = (rows.shape[1], rows.shape[0] * rows.shape[2], rows.shape[3])
    flat = [array.reshape(wide) for array in (master, moment, second)]
    outs = pl.pallas_call(
        update_kernel,
        out_shape=[jax.ShapeDtypeStruct(wide, jnp.float32)] * 3,
        compiler_params=pltpu.CompilerParams(vmem_limit_bytes=16 * 2**20),
    )(rows, *flat)
    return tuple(out.reshape(master.shape) for out in outs)


def update_kernel(rows, master, moment, second, new_master, new_moment, new_second):
    for z in range(8):
        place = (slice(None), pl.ds(z * 8, 8), slice(None))
        grad = rows[z]
        first = first_decay * moment[place] + (1.0 - first_decay) * grad
        square = second_decay * second[place] + (1.0 - second_decay) * grad * grad
        old = master[place]
        update = first / first_fix / (jnp.sqrt(square / second_fix) + epsilon)
        new_moment[place] = first
        new_second[place] = square
        new_master[place] = old - learn_rate * (update + weight_decay * old)


def solution(mesh):
    state = P("tr", ("dp", "tc"), None)
    return jax.shard_map(
        shards,
        mesh=mesh,
        in_specs=(P(("dp", "tc"), "tr"), P(("dp", "tr"), "tc"), state, state, state),
        out_specs=(state, state, state),
        check_vma=False,
    )
```

```python
import jax
import jax.numpy as jnp
from jax import lax
from jax.experimental import pallas as pl
from jax.experimental.pallas import tpu as pltpu
from jax.sharding import PartitionSpec as P

first_decay = 0.9
second_decay = 0.95
learn_rate = 0.0003
weight_decay = 0.1
epsilon = 1e-08
first_fix = 1.0 - 0.9**10
second_fix = 1.0 - 0.95**10

AXES = ("dp", "tr", "tc")
SIDE = 4
ROWS = 48
GROUP = 4
DEPTH = 2
AHEAD = 2 * DEPTH
SOURCES = ((0, 0), (1, 0), (-1, 0), (0, 1))
OWNERS = ((0, 0), (2, 1), (0, 2), (2, 3))
QUARTER = 4 * ROWS


def moves(where):
    pairs = []
    for dp in range(32):
        for tr in range(2):
            for tc in range(4):
                y, x, core, z = where(dp // 8, dp // 2 % 4, dp % 2, 2 * tc + tr)
                to = (y % 4 * 8 + x % 4 * 2 + core % 2, z % 2, z % 8 // 2)
                pairs.append(((dp * 2 + tr) * 4 + tc, (to[0] * 2 + to[1]) * 4 + to[2]))
    return pairs


def send(array, pairs):
    return lax.ppermute(array, AXES, pairs)


OTHER_CORE = moves(lambda y, x, core, z: (y, x, 1 - core, z))
PAIR = moves(lambda y, x, core, z: (y, x, core, z ^ 1))
FEED = [moves(lambda y, x, core, z: (y - dy, x - dx, core, z)) for dx, dy in SOURCES]
REDUCE = [moves(lambda y, x, core, z: (y + dy, x + dx, core, z)) for dx, dy in OWNERS]


def feature_order(activations, half):
    dp = lax.axis_index("dp")
    my_y, my_x, core = dp // 8, dp // 2 % 4, dp % 2
    column = lax.broadcasted_iota(jnp.int32, (1, GROUP * QUARTER), 1)
    row, block = column % ROWS, column // ROWS
    owner, feed = block % 4, block // 4
    target = 1 - core if half else core
    x, y = my_x, my_y
    for index in range(4):
        x = x + jnp.where(owner == index, OWNERS[index][0], 0) - jnp.where(feed == index, SOURCES[index][0], 0)
        y = y + jnp.where(owner == index, OWNERS[index][1], 0) - jnp.where(feed == index, SOURCES[index][1], 0)
    source = (((y + SIDE) % SIDE * SIDE + (x + SIDE) % SIDE) * 2 + target) * ROWS + row
    feature = lax.broadcasted_iota(jnp.int32, (activations.shape[1], column.shape[1]), 0)
    chosen = (feature == source).astype(activations.dtype)
    ordered = lax.dot_general(chosen, activations, (((0,), (1,)), ((), ())), preferred_element_type=jnp.float32)
    return ordered.astype(activations.dtype).reshape(GROUP, QUARTER, activations.shape[0])


def product_kernel(gathered, *refs):
    cots = refs[: 4 * GROUP]
    outs = refs[4 * GROUP : 4 * GROUP + 4]
    act, cot, act_sem, cot_sem = refs[4 * GROUP + 4 :]
    tr = lax.axis_index("tr")
    replicas, quarter, tokens = gathered.shape[1:]
    depth = 4 * tokens

    def copies_of(replica):
        copies = []
        for z in range(8):
            window = pl.ds(replica * depth + z // 2 * tokens, tokens)
            target = act.at[pl.ds(z % 2 * quarter, quarter), window]
            copies.append(pltpu.make_async_copy(gathered.at[z, replica], target, act_sem.at[8 * replica + z]))
        for came in range(2):
            half = 1 - tr if came else tr
            start = pl.multiple_of(replica * depth + half * 2 * tokens, 2 * tokens)
            n = 2 * replica + came
            copies.append(pltpu.make_async_copy(cots[n], cot.at[pl.ds(start, 2 * tokens)], cot_sem.at[n]))
        return copies

    def fetch(replica):
        for copy in copies_of(replica):
            copy.start()

    for replica in range(AHEAD):
        fetch(replica)
    total = None
    for first in range(0, replicas, DEPTH):
        for replica in range(first, first + DEPTH):
            for copy in copies_of(replica):
                copy.wait()
        for replica in range(first + AHEAD, min(first + AHEAD + DEPTH, replicas)):
            fetch(replica)
        window = slice(first * depth, (first + DEPTH) * depth)
        term = jnp.dot(act[:, window], cot[window], preferred_element_type=jnp.float32)
        total = term if total is None else total + term
    total = total.reshape(2, 4, ROWS, total.shape[1])
    for owner in range(4):
        outs[owner][...] = total[:, owner]


def product(gathered, cots):
    replicas, quarter, tokens = gathered.shape[1:]
    units = cots[0].shape[1]
    part = jax.ShapeDtypeStruct((2, ROWS, units), jnp.float32)
    return pl.pallas_call(
        product_kernel,
        in_specs=[pl.BlockSpec(memory_space=pl.ANY)] * (1 + len(cots)),
        out_shape=[part] * 4,
        scratch_shapes=[
            pltpu.VMEM((2 * quarter, replicas * 4 * tokens), gathered.dtype),
            pltpu.VMEM((replicas * 4 * tokens, units), cots[0].dtype),
            pltpu.SemaphoreType.DMA((8 * replicas,)),
            pltpu.SemaphoreType.DMA((2 * replicas,)),
        ],
        compiler_params=pltpu.CompilerParams(vmem_limit_bytes=60 * 2**20),
        cost_estimate=pl.CostEstimate(
            flops=2 * 2 * quarter * replicas * 4 * tokens * units, bytes_accessed=28 * 2**20, transcendentals=0
        ),
    )(gathered, *cots)


def shards(activations, cotangent, master, moment, second):
    tr = lax.axis_index("tr")
    units = cotangent.shape[1] // 2
    other = send(feature_order(activations, 1), OTHER_CORE)
    own = feature_order(activations, 0)
    tokens = cotangent.shape[0]
    away = [
        lax.dynamic_slice(cotangent, (start, (1 - tr) * units), (size, units))
        for start, size in ((0, tokens // 2), (tokens // 2, tokens // 2))
    ]
    own_keep = lax.dynamic_slice_in_dim(cotangent, tr * units, units, 1)
    other, away, own = lax.optimization_barrier((other, away, own))
    first_came, last_came = send(away[0], PAIR), send(away[1], PAIR)
    both = jnp.stack([own, other], axis=1)
    shared = jnp.stack([both[0]] + [send(both[g], FEED[g]) for g in (1, 2, 3)])
    early, shared, first_came = lax.optimization_barrier((own_keep, shared, first_came))
    shared = shared.reshape(2 * GROUP, QUARTER, activations.shape[0])
    gathered = lax.all_gather(shared, ("tc", "tr"), axis=0)
    own_came = jnp.concatenate([first_came, last_came])
    keep = [own_keep] + [send(early, FEED[g]) for g in (1, 2, 3)]
    came = [own_came] + [send(own_came, FEED[g]) for g in (1, 2, 3)]
    cots = []
    for g in range(GROUP):
        cots += [keep[g], came[g], send(keep[g], OTHER_CORE), send(came[g], OTHER_CORE)]
    parts = product(gathered, cots)
    far = [send(parts[owner], REDUCE[owner]) for owner in (1, 3)]
    far.append(send(parts[2], REDUCE[2]))
    rows = parts[0] + far[0] + (far[1] + far[2])
    rows = rows.reshape(2, 4, ROWS // 4, 8, units // 8)
    rows = rows.swapaxes(0, 1).reshape(8, ROWS // 4, 8, units // 8)
    rows = lax.all_to_all(rows, ("tc", "tr"), split_axis=0, concat_axis=0, tiled=True)
    return updated(rows, master, moment, second)


def updated(rows, master, moment, second):
    wide = (rows.shape[1], rows.shape[0] * rows.shape[2], rows.shape[3])
    flat = [array.reshape(wide) for array in (master, moment, second)]
    outs = pl.pallas_call(
        update_kernel,
        out_shape=[jax.ShapeDtypeStruct(wide, jnp.float32)] * 3,
        compiler_params=pltpu.CompilerParams(vmem_limit_bytes=16 * 2**20),
    )(rows, *flat)
    return tuple(out.reshape(master.shape) for out in outs)


def update_kernel(rows, master, moment, second, new_master, new_moment, new_second):
    for z in range(8):
        place = (slice(None), pl.ds(z * 8, 8), slice(None))
        grad = rows[z]
        first = first_decay * moment[place] + (1.0 - first_decay) * grad
        square = second_decay * second[place] + (1.0 - second_decay) * grad * grad
        old = master[place]
        update = first / first_fix / (jnp.sqrt(square / second_fix) + epsilon)
        new_moment[place] = first
        new_second[place] = square
        new_master[place] = old - learn_rate * (update + weight_decay * old)


def solution(mesh):
    state = P("tr", ("dp", "tc"), None)
    return jax.shard_map(
        shards,
        mesh=mesh,
        in_specs=(P(("dp", "tc"), "tr"), P(("dp", "tr"), "tc"), state, state, state),
        out_specs=(state, state, state),
        check_vma=False,
    )
```

```python
import jax
import jax.numpy as jnp
from jax import lax
from jax.experimental import pallas as pl
from jax.experimental.pallas import tpu as pltpu
from jax.sharding import PartitionSpec as P

first_decay = 0.9
second_decay = 0.95
learn_rate = 0.0003
weight_decay = 0.1
epsilon = 1e-08
first_fix = 1.0 - 0.9**10
second_fix = 1.0 - 0.95**10

AXES = ("dp", "tr", "tc")
SIDE = 4
ROWS = 48
GROUP = 4
AHEAD = 3
SOURCES = ((0, 0), (1, 0), (-1, 0), (0, 1))
OWNERS = ((0, 0), (2, 1), (0, 2), (2, 3))
QUARTER = 4 * ROWS


def moves(where):
    pairs = []
    for dp in range(32):
        for tr in range(2):
            for tc in range(4):
                y, x, core, z = where(dp // 8, dp // 2 % 4, dp % 2, 2 * tc + tr)
                to = (y % 4 * 8 + x % 4 * 2 + core % 2, z % 2, z % 8 // 2)
                pairs.append(((dp * 2 + tr) * 4 + tc, (to[0] * 2 + to[1]) * 4 + to[2]))
    return pairs


def send(array, pairs):
    return lax.ppermute(array, AXES, pairs)


OTHER_CORE = moves(lambda y, x, core, z: (y, x, 1 - core, z))
PAIR = moves(lambda y, x, core, z: (y, x, core, z ^ 1))
FEED = [moves(lambda y, x, core, z: (y - dy, x - dx, core, z)) for dx, dy in SOURCES]
REDUCE = [moves(lambda y, x, core, z: (y + dy, x + dx, core, z)) for dx, dy in OWNERS]


def feature_order(activations):
    dp = lax.axis_index("dp")
    my_y, my_x, core = dp // 8, dp // 2 % 4, dp % 2
    column = lax.broadcasted_iota(jnp.int32, (1, 2 * GROUP * QUARTER), 1)
    row, block = column % ROWS, column // ROWS
    owner, feed, half = block % 4, block // 4 % GROUP, block // (4 * GROUP)
    target = jnp.where(half == 0, core, 1 - core)
    x, y = my_x, my_y
    for index in range(4):
        x = x + jnp.where(owner == index, OWNERS[index][0], 0) - jnp.where(feed == index, SOURCES[index][0], 0)
        y = y + jnp.where(owner == index, OWNERS[index][1], 0) - jnp.where(feed == index, SOURCES[index][1], 0)
    source = (((y + SIDE) % SIDE * SIDE + (x + SIDE) % SIDE) * 2 + target) * ROWS + row
    feature = lax.broadcasted_iota(jnp.int32, (activations.shape[1], column.shape[1]), 0)
    chosen = (feature == source).astype(activations.dtype)
    ordered = lax.dot_general(chosen, activations, (((0,), (1,)), ((), ())), preferred_element_type=jnp.float32)
    return ordered.astype(activations.dtype)


def product_kernel(first, gathered, *refs):
    cots = refs[: 4 * GROUP]
    outs = refs[4 * GROUP : 4 * GROUP + 4]
    act, cot, act_sem, cot_sem = refs[4 * GROUP + 4 :]
    tr = lax.axis_index("tr")
    replicas, quarter, tokens = gathered.shape[1:]
    depth = 4 * tokens
    columns = pl.ds(first, cot.shape[1])

    def copies_of(replica):
        copies = []
        for z in range(8):
            window = pl.ds(replica * depth + z // 2 * tokens, tokens)
            target = act.at[pl.ds(z % 2 * quarter, quarter), window]
            copies.append(pltpu.make_async_copy(gathered.at[z, replica], target, act_sem.at[8 * replica + z]))
        for came in range(2):
            half = 1 - tr if came else tr
            start = pl.multiple_of(replica * depth + half * 2 * tokens, 2 * tokens)
            n = 2 * replica + came
            copies.append(pltpu.make_async_copy(cots[n].at[:, columns], cot.at[pl.ds(start, 2 * tokens)], cot_sem.at[n]))
        return copies

    def fetch(replica):
        for copy in copies_of(replica):
            copy.start()

    for replica in range(AHEAD):
        fetch(replica)
    total = None
    for replica in range(replicas):
        if replica + AHEAD < replicas:
            fetch(replica + AHEAD)
        for copy in copies_of(replica):
            copy.wait()
        window = slice(replica * depth, (replica + 1) * depth)
        term = jnp.dot(act[:, window], cot[window], preferred_element_type=jnp.float32)
        total = term if total is None else total + term
    total = total.reshape(2, 4, ROWS, total.shape[1])
    for owner in range(4):
        outs[owner][...] = total[:, owner]


def product(gathered, cots, first, units):
    replicas, quarter, tokens = gathered.shape[1:]
    part = jax.ShapeDtypeStruct((2, ROWS, units), jnp.float32)
    return pl.pallas_call(
        lambda *refs: product_kernel(first, *refs),
        in_specs=[pl.BlockSpec(memory_space=pl.ANY)] * (1 + len(cots)),
        out_shape=[part] * 4,
        scratch_shapes=[
            pltpu.VMEM((2 * quarter, replicas * 4 * tokens), gathered.dtype),
            pltpu.VMEM((replicas * 4 * tokens, units), cots[0].dtype),
            pltpu.SemaphoreType.DMA((8 * replicas,)),
            pltpu.SemaphoreType.DMA((2 * replicas,)),
        ],
        compiler_params=pltpu.CompilerParams(vmem_limit_bytes=60 * 2**20),
        cost_estimate=pl.CostEstimate(
            flops=2 * 2 * quarter * replicas * 4 * tokens * units, bytes_accessed=16 * 2**20, transcendentals=0
        ),
    )(gathered, *cots)


def shards(activations, cotangent, master, moment, second):
    tr = lax.axis_index("tr")
    units = cotangent.shape[1] // 2
    ordered = feature_order(activations).reshape(2, GROUP, QUARTER, activations.shape[0])
    other = send(ordered[1], OTHER_CORE)
    tokens = cotangent.shape[0]
    away = [
        lax.dynamic_slice(cotangent, (start, (1 - tr) * units), (size, units))
        for start, size in ((0, tokens // 2), (tokens // 2, tokens // 2))
    ]
    own_keep = lax.dynamic_slice_in_dim(cotangent, tr * units, units, 1)
    other, away, own_keep = lax.optimization_barrier((other, away, own_keep))
    first_came, last_came = send(away[0], PAIR), send(away[1], PAIR)
    both = jnp.stack([ordered[0], other], axis=1)
    shared = jnp.stack([both[0]] + [send(both[g], FEED[g]) for g in (1, 2, 3)])
    early, shared, first_came = lax.optimization_barrier((own_keep, shared, first_came))
    shared = shared.reshape(2 * GROUP, QUARTER, activations.shape[0])
    gathered = lax.all_gather(shared, ("tc", "tr"), axis=0)
    own_came = jnp.concatenate([first_came, last_came])
    keep = [own_keep] + [send(early, FEED[g]) for g in (1, 2, 3)]
    came = [own_came] + [send(own_came, FEED[g]) for g in (1, 2, 3)]
    cots = []
    for g in range(GROUP):
        cots += [keep[g], came[g], send(keep[g], OTHER_CORE), send(came[g], OTHER_CORE)]
    halves = []
    for first in (0, units // 2):
        parts = product(gathered, cots, first, units // 2)
        far = [send(parts[owner], REDUCE[owner]) for owner in (1, 3, 2)]
        half = parts[0] + far[0] + (far[1] + far[2])
        halves.append(half.reshape(2, 4, ROWS // 4, 4, units // 8))
    rows = jnp.concatenate(halves, axis=3)
    rows = rows.swapaxes(0, 1).reshape(8, ROWS // 4, 8, units // 8)
    rows = lax.all_to_all(rows, ("tc", "tr"), split_axis=0, concat_axis=0, tiled=True)
    return updated(rows, master, moment, second)


def updated(rows, master, moment, second):
    wide = (rows.shape[1], rows.shape[0] * rows.shape[2], rows.shape[3])
    flat = [array.reshape(wide) for array in (master, moment, second)]
    outs = pl.pallas_call(
        update_kernel,
        out_shape=[jax.ShapeDtypeStruct(wide, jnp.float32)] * 3,
        compiler_params=pltpu.CompilerParams(vmem_limit_bytes=16 * 2**20),
    )(rows, *flat)
    return tuple(out.reshape(master.shape) for out in outs)


def update_kernel(rows, master, moment, second, new_master, new_moment, new_second):
    for z in range(8):
        place = (slice(None), pl.ds(z * 8, 8), slice(None))
        grad = rows[z]
        first = first_decay * moment[place] + (1.0 - first_decay) * grad
        square = second_decay * second[place] + (1.0 - second_decay) * grad * grad
        old = master[place]
        update = first / first_fix / (jnp.sqrt(square / second_fix) + epsilon)
        new_moment[place] = first
        new_second[place] = square
        new_master[place] = old - learn_rate * (update + weight_decay * old)


def solution(mesh):
    state = P("tr", ("dp", "tc"), None)
    return jax.shard_map(
        shards,
        mesh=mesh,
        in_specs=(P(("dp", "tc"), "tr"), P(("dp", "tr"), "tc"), state, state, state),
        out_specs=(state, state, state),
        check_vma=False,
    )
```
